32 devices in a mesh: gx: 4 (over z), gy: 2 (over x), gz: 4 (over y, core).
Axes of the slice: x: 2, y: 2, z: 4, core: 2. Of those that a mesh axis runs over, the one named last changes fastest.
Arguments:
- populations: float32 [19, 16, 16, 512], P(None, 'gx', 'gy', 'gz'), may hold values from -0.1 to 0.7
- solid_class: int32 [16, 16, 512], P('gx', 'gy', 'gz'), may hold values from 0 to 3
- part_offset: float32 [512, 3, 128], P(('gx', 'gy', 'gz')), may hold values from -0.5 to 0.5
- part_velocity: float32 [512, 3, 128], P(('gx', 'gy', 'gz')), may hold values from -0.75 to 0.75
- part_drag: float32 [512, 128], P(('gx', 'gy', 'gz')), may hold values from 0.1 to 0.9
- part_cell: int32 [512, 128], P(('gx', 'gy', 'gz')), may hold values from 0 to 4095
- block_rows: int32 [512], P(('gx', 'gy', 'gz')), may hold values from 1 to 128, as said below
- block_dest: int32 [512, 1], P(('gx', 'gy', 'gz')), may hold values from 0 to 3; in each aligned block of 16 rows (0 to 15, 16 to 31, ...) at most 8 rows name the same one
Outputs:
- fluid_velocity: float32 [3, 16, 16, 512], P(None, 'gx', 'gy', 'gz')
- particle_velocity: float32 [1024, 3, 128], P(('gx', 'gy', 'gz'))
The draws below stay inside these ranges and needn't reach their ends.
Inputs may be any that keep to these rules, and one draw needn't show every extreme that they name: Rows 0 to block_rows - 1 of a block hold particles; the first block of every device is full. `block_dest`: among the 16 blocks of one device no target is named more than 8 times, and on some devices one target is named exactly 8 times. `part_cell`: local index (p * 8 + q) * 128 + s of the cell in the target brick.
All inputs are finite; a program needn't handle non-finite values.
Results may differ from the reference program's by a relative error of at most 0.0003.
Values sent between devices are 32-bit elements; how exact they have to be, the bound alone decides.
A program may use at most 128 MiB of HBM per device.

```python
import math
import jax
import jax.numpy as jnp
import numpy as np

CX = 4
CY = 8
CZ = 128
NB_DEV = 16
BLOCK = 128
STEPS = 2
MOST = 8
SLOTS = 32
NX = 16
NY = 16
NZ = 512
BLOCKS = 512
SLOTS_ALL = 1024
N_GX = 4
N_GY = 2
N_GZ = 4
DEVICES = 32


lattice_dirs = np.array([[0, 0, 0], [1, 0, 0], [-1, 0, 0], [0, 1, 0], [0, -1, 0], [0, 0, 1], [0, 0, -1], [1, 1, 0], [-1, -1, 0], [1, -1, 0], [-1, 1, 0], [1, 0, 1], [-1, 0, -1], [1, 0, -1], [-1, 0, 1], [0, 1, 1], [0, -1, -1], [0, 1, -1], [0, -1, 1]], dtype=np.float32)


lattice_weights = np.array([1.0 / 3.0] + [1.0 / 18.0] * 6 + [1.0 / 36.0] * 12, dtype=np.float32)


def draw_populations(key, part):
    subkeys = jax.random.split(key, 3)
    grid_shape = (NX, NY, NZ)
    density = 1.0 + 0.05 * jax.random.uniform(subkeys[0], grid_shape, jnp.float32, -1.0, 1.0)
    velocity = 0.06 * jnp.clip(jax.random.normal(subkeys[1], (3,) + grid_shape, jnp.float32), -2.0, 2.0)
    jitter = 0.1 * jax.random.uniform(subkeys[2], (19,) + grid_shape, jnp.float32, -1.0, 1.0)
    dirs = jnp.asarray(lattice_dirs)
    along_flow = jnp.einsum('id,dxyz->ixyz', dirs, velocity)
    flow_square = jnp.sum(velocity * velocity, axis=0)
    equilibrium = jnp.asarray(lattice_weights).reshape(19, 1, 1, 1) * (density[None] + 3.0 * along_flow + 4.5 * along_flow * along_flow - 1.5 * flow_square[None])
    return (equilibrium * (1.0 + jitter)).astype(jnp.float32)


def draw_block_rows(key, part):
    counted = jax.random.randint(key, (BLOCKS,), 1, BLOCK + 1)
    leading = jnp.arange(BLOCKS) % NB_DEV == 0
    return jnp.where(leading, BLOCK, counted).astype(jnp.int32)


def touch_ends(entries, own_key, smallest, top_value):
    index_at = [jax.random.randint(jax.random.fold_in(own_key, axis), (), 0, length) for axis, length in enumerate(entries.shape)]
    widest = entries.shape.index(max(entries.shape))
    beside = index_at[:widest] + [(index_at[widest] + 1) % entries.shape[widest]] + index_at[widest + 1:]
    return entries.at[tuple(index_at)].set(smallest).at[tuple(beside)].set(top_value)


def block_scale(own_key, shape, cuts, least, high):
    loudness = 1.0
    for position, shards_of in cuts:
        steps = jax.random.uniform(jax.random.fold_in(jax.random.fold_in(own_key, 6), position), (shards_of,), jnp.float32, least / len(cuts), high / len(cuts))
        loudness = loudness * jnp.repeat(jnp.exp(steps), shape[position] // shards_of).reshape((-1,) + (1,) * (len(shape) - 1 - position))
    return loudness


def routed_block(own_key, own, number, rows, amount, top, limit, skew):
    ranking = jax.random.permutation(own_key, amount)
    heavy_load, usual = shares(amount, rows * top, limit, skew, True), shares(amount, rows * top, limit, skew, False)
    places = jnp.arange(amount)

    def named(lengths, offset_by):
        used = int((lengths > 0).sum())
        fixed = max(1, used // 4)
        passed = fixed + (places - fixed + offset_by * (used - fixed)) % max(1, amount - fixed)
        return jnp.zeros((amount,), jnp.int32).at[ranking[jnp.where(places < fixed, places, passed)]].set(jnp.asarray(lengths, jnp.int32))

    lengths = jnp.where(number % 4 == 0, named(heavy_load, number // 4), named(usual, number - number // 4 - 1))
    mixed = jax.random.permutation(jax.random.fold_in(own, 3), amount)
    giver, sink = mixed[0:amount // 2 * 2:2], mixed[1:amount // 2 * 2:2]
    margin = jnp.minimum(lengths[giver] - 1, limit - lengths[sink]) // 2
    margin = jnp.where((giver == ranking[0]) | (sink == ranking[0]) | (lengths[sink] == 0), 0, jnp.maximum(margin, 0))
    passed = jax.random.randint(jax.random.fold_in(own, 4), (amount // 2,), 0, 1 << 20) % (margin + 1)
    lengths = lengths.at[giver].add(-passed).at[sink].add(passed)
    labels = jnp.searchsorted(jnp.cumsum(lengths), jnp.arange(rows * top), side="right").astype(jnp.int32)
    listing = labels.reshape(top, rows).T
    listing = listing[jax.random.permutation(jax.random.fold_in(own, 1), rows)]
    offset_by = jax.random.randint(jax.random.fold_in(own, 2), (rows, 1), 0, top)
    return jnp.take_along_axis(listing, (jnp.arange(top)[None, :] + offset_by) % top, axis=1)


def shares(amount, total, bound, lean, full):
    weights = [(1 << 20) // math.isqrt(grade ** lean) + 1 for grade in range(1, amount + 1)]
    largest = bound if full else min(bound, max(-(-total // amount), total * weights[0] // sum(weights)))
    least = 1 if total - largest >= amount - 1 else 0
    given, surplus = [largest] + [least] * (amount - 1), total - largest - least * (amount - 1)
    while surplus > 0:
        movable = [i for i in range(1, amount) if given[i] < largest] or [i for i in range(1, amount) if given[i] < bound]
        mass, budget = sum([weights[i] for i in movable]), surplus
        for i in movable:
            extra = min(bound - given[i], max(1, budget * weights[i] // mass), surplus)
            given[i] = given[i] + extra
            surplus = surplus - extra
    return np.array(given)


def centred(own_key, extent, scale, most, shards=(), held_as=jnp.bfloat16):
    entries = jax.random.normal(own_key, extent, jnp.float32) * scale
    if len(shards) > 0:
        entries = block_scale(own_key, extent, shards, -0.22, 0.18) * entries
    return jnp.clip(entries, min=-most, max=most).astype(held_as)


def setup_inputs(seed: int = 0) -> dict:
    key_of = jax.random.split(jax.random.key(seed), 9)
    populations = draw_populations(jax.random.fold_in(key_of[8], 71), 0)
    solid_class = touch_ends(jax.random.randint(key_of[1], (NX, NY, NZ), 0, 4), jax.random.fold_in(key_of[1], 1), 0, 3).astype(jnp.int32)
    part_offset = jnp.clip(jax.random.uniform(key_of[2], (BLOCKS, 3, BLOCK), jnp.float32, -0.5, 0.5) * block_scale(key_of[2], (BLOCKS, 3, BLOCK), ((0, 32),), -0.4, 0.0), -0.5, 0.5)
    part_velocity = centred(key_of[3], (BLOCKS, 3, BLOCK), 0.05, 0.75, ((0, 32),), jnp.float32)
    part_drag = jnp.clip(jnp.exp(math.log(0.9) - 2.1972245 * jax.random.uniform(key_of[4], (BLOCKS, BLOCK), jnp.float32) ** block_scale(key_of[4], (BLOCKS, BLOCK), ((0, 32),), -0.2, 0.2)), 0.1, 0.9)
    part_cell = touch_ends(jax.random.randint(key_of[5], (BLOCKS, BLOCK), 0, CX * CY * CZ), jax.random.fold_in(key_of[5], 1), 0, (CX * CY * CZ) - 1).astype(jnp.int32)
    block_rows = draw_block_rows(jax.random.fold_in(key_of[8], 71), 0)
    block_dest_keys = jax.random.split(jax.random.fold_in(key_of[7], 1), BLOCKS // NB_DEV)
    block_dest_turns = jax.random.permutation(jax.random.fold_in(key_of[7], 3), BLOCKS // NB_DEV)
    block_dest = jax.vmap(lambda own, number: routed_block(jax.random.fold_in(key_of[7], 2), own, number, NB_DEV, N_GX, 1, MOST, 2))(block_dest_keys, block_dest_turns).reshape((BLOCKS, 1))
    return dict(populations=populations, solid_class=solid_class, part_offset=part_offset, part_velocity=part_velocity, part_drag=part_drag, part_cell=part_cell, block_rows=block_rows, block_dest=block_dest)


directions = ((0, 0, 0), (1, 0, 0), (-1, 0, 0), (0, 1, 0), (0, -1, 0), (0, 0, 1), (0, 0, -1),
              (1, 1, 0), (-1, -1, 0), (1, -1, 0), (-1, 1, 0), (1, 0, 1), (-1, 0, -1),
              (1, 0, -1), (-1, 0, 1), (0, 1, 1), (0, -1, -1), (0, 1, -1), (0, -1, 1))
weights = (1.0 / 3.0,) + (1.0 / 18.0,) * 6 + (1.0 / 36.0,) * 12
opposite = (0, 2, 1, 4, 3, 6, 5, 8, 7, 10, 9, 12, 11, 14, 13, 16, 15, 18, 17)
relax_rate = 1.25
speed_unit = 0.05


def project(vector, direction):
    summed = None
    for d in range(3):
        if direction[d] != 0:
            signed = vector[d] if direction[d] > 0 else -vector[d]
            summed = signed if summed is None else summed + signed
    return summed


def moments(fields):
    density = fields[0]
    for i in range(1, 19):
        density = density + fields[i]
    components = []
    for d in range(3):
        summed = None
        for i in range(1, 19):
            if directions[i][d] != 0:
                signed = fields[i] if directions[i][d] > 0 else -fields[i]
                summed = signed if summed is None else summed + signed
        components.append(summed)
    return density, jnp.stack(components)


def collide(fields, density, velocity, cell_force, gray_fraction):
    flow_square = velocity[0] * velocity[0] + velocity[1] * velocity[1] + velocity[2] * velocity[2]
    post_list = []
    for i in range(19):
        baseline = density - 1.5 * flow_square
        if i > 0:
            along_flow = project(velocity, directions[i])
            along_force = project(cell_force, directions[i])
            baseline = baseline + 3.0 * along_flow + 4.5 * along_flow * along_flow
        equilibrium = weights[i] * baseline
        relaxed = fields[i] + relax_rate * (equilibrium - fields[i])
        if i > 0:
            relaxed = relaxed + 3.0 * weights[i] * along_force
        post_list.append((1.0 - gray_fraction) * relaxed + gray_fraction * fields[opposite[i]])
    return post_list


def corner_table(places, offset, extents, wrapped):
    options = []
    for d in range(3):
        displace = offset[:, d, :]
        step_sign = jnp.where(displace >= 0.0, 1, -1).astype(jnp.int32)
        nearer = places[d]
        farther = places[d] + step_sign
        if wrapped:
            farther = farther % extents[d]
        options.append(((nearer, 1.0 - jnp.abs(displace)), (farther, jnp.abs(displace))))
    corners = []
    for a in options[0]:
        for b in options[1]:
            for c in options[2]:
                flat_index = ((a[0] * extents[1] + b[0]) * extents[2] + c[0]).astype(jnp.int32)
                corners.append((flat_index, a[1] * b[1] * c[1]))
    return corners


def reference(populations, solid_class, part_offset, part_velocity, part_drag, part_cell, block_rows, block_dest):
    gray_fraction = solid_class.astype(jnp.float32) * 0.25
    destination = block_dest[:, 0].astype(jnp.int32)
    block_ids = jnp.arange(BLOCKS, dtype=jnp.int32)
    device = block_ids // NB_DEV
    brick_x = device // (N_GY * N_GZ)
    brick_y = (device // N_GZ) % N_GY
    brick_z = device % N_GZ
    p = part_cell // (CY * CZ)
    q = (part_cell // CZ) % CY
    s = part_cell % CZ
    place_x = (destination[:, None] * CX + p).astype(jnp.int32)
    place_y = (brick_y[:, None] * CY + q).astype(jnp.int32)
    place_z = (brick_z[:, None] * CZ + s).astype(jnp.int32)
    corners = corner_table((place_x, place_y, place_z), part_offset, (NX, NY, NZ), True)
    live_rows = jnp.arange(BLOCK, dtype=jnp.int32)[None, :] < block_rows[:, None]
    velocity = part_velocity
    fields = populations
    for repeat in range(STEPS):
        density, flow = moments(fields)
        flattened = flow.reshape(3, -1)
        sampled = jnp.zeros_like(velocity)
        for flat_index, weight in corners:
            sampled = sampled + weight[:, None, :] * jnp.moveaxis(flattened[:, flat_index], 0, 1)
        drag_force = jnp.where(live_rows[:, None, :], part_drag[:, None, :] * (sampled - velocity), 0.0)
        velocity = velocity + drag_force
        spread = jnp.zeros_like(flattened)
        for flat_index, weight in corners:
            spread = spread.at[:, flat_index].add(jnp.moveaxis(-weight[:, None, :] * drag_force, 1, 0))
        cell_force = spread.reshape(3, NX, NY, NZ)
        post_list = collide(fields, density, flow, cell_force, gray_fraction)
        fields = jnp.stack([jnp.roll(post_list[i], directions[i], axis=(0, 1, 2)) for i in range(19)])
        post_list = None
    density, flow = moments(fields)
    fluid_velocity = flow / speed_unit
    onehot = (destination.reshape(DEVICES, NB_DEV)[:, :, None] == jnp.arange(N_GX, dtype=jnp.int32)[None, None, :]).astype(jnp.int32)
    before = (jnp.cumsum(onehot, axis=1) - onehot).astype(jnp.int32)
    block_rank = jnp.sum(before * onehot, axis=2).reshape(BLOCKS).astype(jnp.int32)
    target = (destination * N_GY + brick_y) * N_GZ + brick_z
    slot_index = (target * SLOTS + brick_x * MOST + block_rank).astype(jnp.int32)
    shown = jnp.where(live_rows[:, None, :], velocity / speed_unit, 0.0)
    particle_velocity = jnp.zeros((SLOTS_ALL, 3, BLOCK), jnp.float32).at[slot_index].set(shown)
    return fluid_velocity, particle_velocity
```

```python
import jax
import jax.numpy as jnp
from jax import lax
from jax.sharding import PartitionSpec as P

STEPS = 2


directions = (
    (0, 0, 0),
    (1, 0, 0),
    (-1, 0, 0),
    (0, 1, 0),
    (0, -1, 0),
    (0, 0, 1),
    (0, 0, -1),
    (1, 1, 0),
    (-1, -1, 0),
    (1, -1, 0),
    (-1, 1, 0),
    (1, 0, 1),
    (-1, 0, -1),
    (1, 0, -1),
    (-1, 0, 1),
    (0, 1, 1),
    (0, -1, -1),
    (0, 1, -1),
    (0, -1, 1),
)
weights = (1.0 / 3.0,) + (1.0 / 18.0,) * 6 + (1.0 / 36.0,) * 12
opposite = (0, 2, 1, 4, 3, 6, 5, 8, 7, 10, 9, 12, 11, 14, 13, 16, 15, 18, 17)
relax_rate = 1.25
speed_unit = 0.05


def with_halo(cells, sides, width):
    for axis, dim in sides:
        count = lax.axis_size(axis)
        head = lax.slice_in_dim(cells, 0, width, axis=dim)
        tail = lax.slice_in_dim(cells, cells.shape[dim] - width, cells.shape[dim], axis=dim)
        cells = jnp.concatenate(
            [
                lax.ppermute(tail, axis, [(i, (i + 1) % count) for i in range(count)]),
                cells,
                lax.ppermute(head, axis, [((i + 1) % count, i) for i in range(count)]),
            ],
            axis=dim,
        )
    return cells


def project(vector, direction):
    summed = None
    for d in range(3):
        if direction[d] != 0:
            signed = vector[d] if direction[d] > 0 else -vector[d]
            summed = signed if summed is None else summed + signed
    return summed


def moments(fields):
    density = fields[0]
    for i in range(1, 19):
        density = density + fields[i]
    components = []
    for d in range(3):
        summed = None
        for i in range(1, 19):
            if directions[i][d] != 0:
                signed = fields[i] if directions[i][d] > 0 else -fields[i]
                summed = signed if summed is None else summed + signed
        components.append(summed)
    return (density, jnp.stack(components))


def collide(fields, density, velocity, cell_force, gray_fraction):
    flow_square = velocity[0] * velocity[0] + velocity[1] * velocity[1] + velocity[2] * velocity[2]
    post_list = []
    for i in range(19):
        baseline = density - 1.5 * flow_square
        if i > 0:
            along_flow = project(velocity, directions[i])
            along_force = project(cell_force, directions[i])
            baseline = baseline + 3.0 * along_flow + 4.5 * along_flow * along_flow
        equilibrium = weights[i] * baseline
        relaxed = fields[i] + relax_rate * (equilibrium - fields[i])
        if i > 0:
            relaxed = relaxed + 3.0 * weights[i] * along_force
        post_list.append((1.0 - gray_fraction) * relaxed + gray_fraction * fields[opposite[i]])
    return post_list


def fold_ghost(widened, dim):
    length = widened.shape[dim] - 4
    folded = lax.slice_in_dim(widened, 2, length + 2, axis=dim)
    lower = lax.slice_in_dim(widened, 0, 1, axis=dim)
    upper = lax.slice_in_dim(widened, length + 3, length + 4, axis=dim)
    lower_pad = [(0, 0)] * 4
    upper_pad = [(0, 0)] * 4
    lower_pad[dim] = (0, length - 1)
    upper_pad[dim] = (length - 1, 0)
    return folded + jnp.pad(lower, lower_pad) + jnp.pad(upper, upper_pad)


def move_layers(layers, moving, widened, dim):
    for k, i in enumerate(moving):
        extent = layers[i].shape[dim]
        start = 1 - directions[i][dim]
        layers[i] = lax.slice_in_dim(widened[k], start, start + extent, axis=dim)
    return layers


def propagate_by_axis(post_list):
    layers = list(post_list)
    moving = [i for i in range(19) if directions[i][0] != 0]
    widened = with_halo(jnp.stack([layers[i] for i in moving]), (("gx", 1),), 1)
    layers = move_layers(layers, moving, widened, 0)
    moving = [i for i in range(19) if directions[i][1] != 0]
    widened = with_halo(jnp.stack([layers[i] for i in moving]), (("gy", 2),), 1)
    layers = move_layers(layers, moving, widened, 1)
    moving = [i for i in range(19) if directions[i][2] != 0]
    widened = with_halo(jnp.stack([layers[i] for i in moving]), (("gz", 3),), 1)
    layers = move_layers(layers, moving, widened, 2)
    return layers


def per_device(
    populations,
    solid_class,
    part_offset,
    part_velocity,
    part_drag,
    part_cell,
    block_rows,
    block_dest,
):
    size_x, size_y, size_z = (populations.shape[1], populations.shape[2], populations.shape[3])
    rows_block = part_cell.shape[1]
    block_count = block_dest.shape[0]
    peers = lax.axis_size("gx")
    capacity = 2 * block_count // peers
    slot_count = peers * capacity
    destination = block_dest[:, 0]
    onehot = (destination[:, None] == jnp.arange(peers, dtype=jnp.int32)[None, :]).astype(jnp.int32)
    before = jnp.cumsum(onehot, axis=0) - onehot
    block_rank = jnp.sum(before * onehot, axis=1)
    slot_index = destination * capacity + block_rank
    match = slot_index[None, :] == jnp.arange(slot_count, dtype=jnp.int32)[:, None]
    filled = jnp.any(match, axis=1)
    source = jnp.sum(jnp.where(match, jnp.arange(block_count, dtype=jnp.int32)[None, :], 0), axis=1)
    floats = jnp.concatenate([part_offset, part_velocity, part_drag[:, None, :]], axis=1)
    send_floats = jnp.where(filled[:, None, None], jnp.take(floats, source, axis=0), 0.0)
    send_cells = jnp.where(filled[:, None], jnp.take(part_cell, source, axis=0), 0)
    send_rows = jnp.where(filled, jnp.take(block_rows, source, axis=0), 0)
    got_floats, got_cells, got_rows = (
        lax.all_to_all(send_floats, "gx", split_axis=0, concat_axis=0, tiled=True),
        lax.all_to_all(send_cells, "gx", split_axis=0, concat_axis=0, tiled=True),
        lax.all_to_all(send_rows, "gx", split_axis=0, concat_axis=0, tiled=True),
    )
    offset = got_floats[:, 0:3, :]
    velocity = got_floats[:, 3:6, :]
    drag_rate = got_floats[:, 6, :]
    live_rows = jnp.arange(rows_block, dtype=jnp.int32)[None, :] < got_rows[:, None]
    p = got_cells // (size_y * size_z) + 1
    q = got_cells // size_z % size_y + 1
    s = got_cells % size_z + 1
    slots = offset.shape[0]
    tables = []
    for d, (place, extent) in enumerate(((p, size_x + 2), (q, size_y + 2), (s, size_z + 2))):
        displace = offset[:, d, :].reshape(-1)
        nearer = place.reshape(-1)
        farther = nearer + jnp.where(displace >= 0.0, 1, -1).astype(jnp.int32)
        grid = jnp.arange(extent, dtype=jnp.int32)[None, :]
        tables.append(
            jnp.where(grid == nearer[:, None], (1.0 - jnp.abs(displace))[:, None], 0.0)
            + jnp.where(grid == farther[:, None], jnp.abs(displace)[:, None], 0.0)
        )
    across = (tables[0][:, :, None] * tables[1][:, None, :]).reshape(slots * rows_block, -1)
    gray_fraction = solid_class.astype(jnp.float32) * 0.25
    fields = populations
    for repeat in range(STEPS):
        density, flow = moments(fields)
        rim_field = with_halo(flow, (("gx", 1), ("gy", 2), ("gz", 3)), 1)
        lines = rim_field.reshape(3, -1, size_z + 2)
        along = jnp.einsum("nz,dkz->dnk", tables[2], lines, precision=lax.Precision.HIGHEST)
        sampled = jnp.sum(along * across[None], axis=2).reshape(3, slots, rows_block)
        sampled = jnp.moveaxis(sampled, 0, 1)
        drag_force = jnp.where(
            live_rows[:, None, :], drag_rate[:, None, :] * (sampled - velocity), 0.0
        )
        velocity = velocity + drag_force
        pushed = -jnp.moveaxis(drag_force, 1, 0).reshape(3, -1)
        ghosts = jnp.einsum(
            "dnk,nz->dkz", pushed[:, :, None] * across[None], tables[2],
            precision=lax.Precision.HIGHEST,
        )
        ghosts = ghosts.reshape(3, size_x + 2, size_y + 2, size_z + 2)
        widened = with_halo(ghosts, (("gx", 1), ("gy", 2), ("gz", 3)), 1)
        cell_force = fold_ghost(fold_ghost(fold_ghost(widened, 1), 2), 3)
        post_list = collide(fields, density, flow, cell_force, gray_fraction)
        fields = jnp.stack(propagate_by_axis(post_list))
    density, flow = moments(fields)
    fluid_velocity = flow / speed_unit
    particle_velocity = jnp.where(live_rows[:, None, :], velocity / speed_unit, 0.0)
    return (fluid_velocity, particle_velocity)


def solution(mesh):
    in_specs = (
        P(None, "gx", "gy", "gz"),
        P("gx", "gy", "gz"),
        P(("gx", "gy", "gz"), None, None),
        P(("gx", "gy", "gz"), None, None),
        P(("gx", "gy", "gz"), None),
        P(("gx", "gy", "gz"), None),
        P(("gx", "gy", "gz")),
        P(("gx", "gy", "gz"), None),
    )
    out_specs = (P(None, "gx", "gy", "gz"), P(("gx", "gy", "gz"), None, None))
    return jax.shard_map(
        per_device, mesh=mesh, in_specs=in_specs, out_specs=out_specs, check_vma=False
    )
```

```python
import jax
import jax.numpy as jnp
from jax import lax
from jax.sharding import PartitionSpec as P

STEPS = 2


directions = (
    (0, 0, 0),
    (1, 0, 0),
    (-1, 0, 0),
    (0, 1, 0),
    (0, -1, 0),
    (0, 0, 1),
    (0, 0, -1),
    (1, 1, 0),
    (-1, -1, 0),
    (1, -1, 0),
    (-1, 1, 0),
    (1, 0, 1),
    (-1, 0, -1),
    (1, 0, -1),
    (-1, 0, 1),
    (0, 1, 1),
    (0, -1, -1),
    (0, 1, -1),
    (0, -1, 1),
)
weights = (1.0 / 3.0,) + (1.0 / 18.0,) * 6 + (1.0 / 36.0,) * 12
opposite = (0, 2, 1, 4, 3, 6, 5, 8, 7, 10, 9, 12, 11, 14, 13, 16, 15, 18, 17)
relax_rate = 1.25
speed_unit = 0.05


def swap(axis, onward, backward):
    count = lax.axis_size(axis)
    if count == 2:
        both = lax.ppermute(jnp.stack([onward, backward]), axis, [(0, 1), (1, 0)])
        return (both[0], both[1])
    return (
        lax.ppermute(onward, axis, [(i, (i + 1) % count) for i in range(count)]),
        lax.ppermute(backward, axis, [((i + 1) % count, i) for i in range(count)]),
    )


def with_halo(cells, sides, width):
    for axis, dim in sides:
        length = cells.shape[dim]
        head = lax.slice_in_dim(cells, 0, width, axis=dim)
        tail = lax.slice_in_dim(cells, length - width, length, axis=dim)
        before, after = swap(axis, tail, head)
        cells = jnp.concatenate([before, cells, after], axis=dim)
    return cells


def spread_sums(ghosts, sides, width):
    for axis, dim in sides:
        length = ghosts.shape[dim]
        head = lax.slice_in_dim(ghosts, 0, width + 1, axis=dim)
        tail = lax.slice_in_dim(ghosts, length - width - 1, length, axis=dim)
        before, after = swap(axis, tail, head)
        around = [(0, 0)] * 4
        around[dim] = (width - 1, width - 1)
        low, high = list(around), list(around)
        rest = length + 2 * (width - 1) - (width + 1)
        low[dim] = (0, rest)
        high[dim] = (rest, 0)
        ghosts = jnp.pad(ghosts, around) + jnp.pad(before, low) + jnp.pad(after, high)
    return ghosts


def project(vector, direction):
    summed = None
    for d in range(3):
        if direction[d] != 0:
            signed = vector[d] if direction[d] > 0 else -vector[d]
            summed = signed if summed is None else summed + signed
    return summed


def moments(fields):
    density = fields[0]
    for i in range(1, 19):
        density = density + fields[i]
    components = []
    for d in range(3):
        summed = None
        for i in range(1, 19):
            if directions[i][d] != 0:
                signed = fields[i] if directions[i][d] > 0 else -fields[i]
                summed = signed if summed is None else summed + signed
        components.append(summed)
    return (density, jnp.stack(components))


def collide(fields, density, velocity, cell_force, gray_fraction):
    flow_square = velocity[0] * velocity[0] + velocity[1] * velocity[1] + velocity[2] * velocity[2]
    post_list = []
    for i in range(19):
        baseline = density - 1.5 * flow_square
        if i > 0:
            along_flow = project(velocity, directions[i])
            along_force = project(cell_force, directions[i])
            baseline = baseline + 3.0 * along_flow + 4.5 * along_flow * along_flow
        equilibrium = weights[i] * baseline
        relaxed = fields[i] + relax_rate * (equilibrium - fields[i])
        if i > 0:
            relaxed = relaxed + 3.0 * weights[i] * along_force
        post_list.append((1.0 - gray_fraction) * relaxed + gray_fraction * fields[opposite[i]])
    return post_list


def propagate(post_list):
    moved = []
    for i in range(19):
        layer = post_list[i]
        for dim in range(3):
            start = 1 - directions[i][dim]
            layer = lax.slice_in_dim(layer, start, start + layer.shape[dim] - 2, axis=dim)
        moved.append(layer)
    return moved


def per_device(
    populations,
    solid_class,
    part_offset,
    part_velocity,
    part_drag,
    part_cell,
    block_rows,
    block_dest,
):
    size_x, size_y, size_z = (populations.shape[1], populations.shape[2], populations.shape[3])
    rows_block = part_cell.shape[1]
    block_count = block_dest.shape[0]
    peers = lax.axis_size("gx")
    capacity = 2 * block_count // peers
    slot_count = peers * capacity
    destination = block_dest[:, 0]
    onehot = (destination[:, None] == jnp.arange(peers, dtype=jnp.int32)[None, :]).astype(jnp.int32)
    before = jnp.cumsum(onehot, axis=0) - onehot
    block_rank = jnp.sum(before * onehot, axis=1)
    slot_index = destination * capacity + block_rank
    match = slot_index[None, :] == jnp.arange(slot_count, dtype=jnp.int32)[:, None]
    filled = jnp.any(match, axis=1)
    source = jnp.sum(jnp.where(match, jnp.arange(block_count, dtype=jnp.int32)[None, :], 0), axis=1)
    alive = jnp.arange(rows_block, dtype=jnp.int32)[None, :] < block_rows[:, None]
    named = jnp.where(alive, part_cell, -1).astype(jnp.float32)
    floats = jnp.concatenate(
        [part_offset, part_velocity, part_drag[:, None, :], named[:, None, :]], axis=1
    )
    empty = jnp.where(jnp.arange(8) == 7, -1.0, 0.0).astype(jnp.float32)[None, :, None]
    send_floats = jnp.where(filled[:, None, None], jnp.take(floats, source, axis=0), empty)
    got_floats = lax.all_to_all(send_floats, "gx", split_axis=0, concat_axis=0, tiled=True)
    offset = got_floats[:, 0:3, :]
    velocity = got_floats[:, 3:6, :]
    drag_rate = got_floats[:, 6, :]
    live_rows = got_floats[:, 7, :] >= 0.0
    got_cells = jnp.maximum(got_floats[:, 7, :], 0.0).astype(jnp.int32)
    p = got_cells // (size_y * size_z) + 1
    q = got_cells // size_z % size_y + 1
    s = got_cells % size_z + 1
    slots = offset.shape[0]
    tables = []
    for d, (place, extent) in enumerate(((p, size_x + 2), (q, size_y + 2), (s, size_z + 2))):
        displace = offset[:, d, :].reshape(-1)
        nearer = place.reshape(-1)
        farther = nearer + jnp.where(displace >= 0.0, 1, -1).astype(jnp.int32)
        grid = jnp.arange(extent, dtype=jnp.int32)[None, :]
        tables.append(
            jnp.where(grid == nearer[:, None], (1.0 - jnp.abs(displace))[:, None], 0.0)
            + jnp.where(grid == farther[:, None], jnp.abs(displace)[:, None], 0.0)
        )
    across = (tables[0][:, :, None] * tables[1][:, None, :]).reshape(slots * rows_block, -1)
    sides = (("gz", 3), ("gx", 1), ("gy", 2))
    gray = solid_class.astype(jnp.float32) * 0.25
    wide = with_halo(jnp.concatenate([populations, gray[None]]), sides, STEPS)
    fields = [wide[i] for i in range(19)]
    gray_fraction = wide[19]
    for repeat in range(STEPS):
        reach = STEPS - repeat
        density, flow = moments(fields)
        near = flow
        for d, size in enumerate((size_x, size_y, size_z)):
            near = lax.slice_in_dim(near, reach - 1, reach + 1 + size, axis=d + 1)
        lines = near.reshape(3, -1, size_z + 2)
        along = jnp.einsum("nz,dkz->dnk", tables[2], lines, precision=lax.Precision.HIGH)
        sampled = jnp.sum(along * across[None], axis=2).reshape(3, slots, rows_block)
        sampled = jnp.moveaxis(sampled, 0, 1)
        drag_force = jnp.where(
            live_rows[:, None, :], drag_rate[:, None, :] * (sampled - velocity), 0.0
        )
        velocity = velocity + drag_force
        pushed = -jnp.moveaxis(drag_force, 1, 0).reshape(3, -1)
        ghosts = jnp.einsum(
            "dnk,nz->dkz", pushed[:, :, None] * across[None], tables[2],
            precision=lax.Precision.HIGH,
        )
        ghosts = ghosts.reshape(3, size_x + 2, size_y + 2, size_z + 2)
        cell_force = spread_sums(ghosts, sides, reach)
        post_list = collide(fields, density, flow, cell_force, gray_fraction)
        fields = propagate(post_list)
        gray_fraction = gray_fraction[1:-1, 1:-1, 1:-1]
    density, flow = moments(fields)
    fluid_velocity = flow / speed_unit
    particle_velocity = jnp.where(live_rows[:, None, :], velocity / speed_unit, 0.0)
    return (fluid_velocity, particle_velocity)


def solution(mesh):
    in_specs = (
        P(None, "gx", "gy", "gz"),
        P("gx", "gy", "gz"),
        P(("gx", "gy", "gz"), None, None),
        P(("gx", "gy", "gz"), None, None),
        P(("gx", "gy", "gz"), None),
        P(("gx", "gy", "gz"), None),
        P(("gx", "gy", "gz")),
        P(("gx", "gy", "gz"), None),
    )
    out_specs = (P(None, "gx", "gy", "gz"), P(("gx", "gy", "gz"), None, None))
    return jax.shard_map(
        per_device, mesh=mesh, in_specs=in_specs, out_specs=out_specs, check_vma=False
    )
```

```python
import functools

import jax
import jax.numpy as jnp
from jax import lax
from jax.experimental import pallas as pl
from jax.experimental.pallas import tpu as pltpu
from jax.sharding import PartitionSpec as P

STEPS = 2


directions = (
    (0, 0, 0),
    (1, 0, 0),
    (-1, 0, 0),
    (0, 1, 0),
    (0, -1, 0),
    (0, 0, 1),
    (0, 0, -1),
    (1, 1, 0),
    (-1, -1, 0),
    (1, -1, 0),
    (-1, 1, 0),
    (1, 0, 1),
    (-1, 0, -1),
    (1, 0, -1),
    (-1, 0, 1),
    (0, 1, 1),
    (0, -1, -1),
    (0, 1, -1),
    (0, -1, 1),
)
weights = (1.0 / 3.0,) + (1.0 / 18.0,) * 6 + (1.0 / 36.0,) * 12
opposite = (0, 2, 1, 4, 3, 6, 5, 8, 7, 10, 9, 12, 11, 14, 13, 16, 15, 18, 17)
relax_rate = 1.25
speed_unit = 0.05


AXES = ("gx", "gy", "gz")
MESH = pl.DeviceIdType.MESH


def neighbour(axis, step):
    place = [lax.axis_index(name) for name in AXES]
    count = lax.axis_size(axis)
    where = AXES.index(axis)
    place[where] = lax.rem(place[where] + count + step, count)
    return tuple(place)


def greet():
    barrier = pltpu.get_barrier_semaphore()
    for axis in AXES:
        for step in (1, -1):
            pl.semaphore_signal(barrier, inc=1, device_id=neighbour(axis, step), device_id_type=MESH)
    pl.semaphore_wait(barrier, 6)


def swap(axis, sources, targets, send_sems, recv_sems):
    copies = []
    for k, step in enumerate((1, -1)):
        number = 2 * AXES.index(axis) + k
        copy = pltpu.make_async_remote_copy(
            src_ref=sources[k],
            dst_ref=targets[k],
            send_sem=send_sems.at[number],
            recv_sem=recv_sems.at[number],
            device_id=neighbour(axis, step),
            device_id_type=MESH,
        )
        copy.start()
        copies.append(copy)
    for copy in copies:
        copy.wait()


def widen_kernel(width, cells, out, y_out, y_in, mid, z_out, z_in, send_sems, recv_sems):
    fields, size_x, size_y, size_z = cells.shape
    greet()
    y_out[0] = cells[:, :, size_y - width :, :]
    y_out[1] = cells[:, :, :width, :]
    swap("gy", (y_out.at[0], y_out.at[1]), (y_in.at[0], y_in.at[1]), send_sems, recv_sems)
    mid[:, width : width + size_x] = jnp.concatenate([y_in[0], cells[...], y_in[1]], axis=2)
    swap(
        "gx",
        (mid.at[:, pl.ds(size_x, width)], mid.at[:, pl.ds(width, width)]),
        (mid.at[:, pl.ds(0, width)], mid.at[:, pl.ds(size_x + width, width)]),
        send_sems,
        recv_sems,
    )
    z_out[0] = jnp.concatenate([mid[c, :, :, size_z - width :] for c in range(fields)], axis=-1)
    z_out[1] = jnp.concatenate([mid[c, :, :, :width] for c in range(fields)], axis=-1)
    swap("gz", (z_out.at[0], z_out.at[1]), (z_in.at[0], z_in.at[1]), send_sems, recv_sems)
    for c in range(fields):
        cut = slice(c * width, (c + 1) * width)
        out[c] = jnp.concatenate([z_in[0, :, :, cut], mid[c], z_in[1, :, :, cut]], axis=-1)


def call_kernel(kernel, operand, out_shape, scratch, number):
    return pl.pallas_call(
        kernel,
        out_shape=jax.ShapeDtypeStruct(out_shape, jnp.float32),
        in_specs=[pl.BlockSpec(memory_space=pltpu.VMEM)],
        out_specs=pl.BlockSpec(memory_space=pltpu.VMEM),
        scratch_shapes=[pltpu.VMEM(shape, jnp.float32) for shape in scratch]
        + [pltpu.SemaphoreType.DMA((6,)), pltpu.SemaphoreType.DMA((6,))],
        compiler_params=pltpu.CompilerParams(
            collective_id=number, has_side_effects=True, vmem_limit_bytes=40 * 1024 * 1024
        ),
    )(operand)


def with_halo(cells, width):
    fields, size_x, size_y, size_z = cells.shape
    wide_x, wide_y, wide_z = (size_x + 2 * width, size_y + 2 * width, size_z + 2 * width)
    y_slab = (2, fields, size_x, width, size_z)
    z_slab = (2, wide_x, wide_y, fields * width)
    return call_kernel(
        functools.partial(widen_kernel, width),
        cells,
        (fields, wide_x, wide_y, wide_z),
        [y_slab, y_slab, (fields, wide_x, wide_y, size_z), z_slab, z_slab],
        0,
    )


def add_ends(middle, before, after, dim, width):
    length = middle.shape[dim]
    part = functools.partial(lax.slice_in_dim, axis=dim)
    if width == 1:
        pieces = [
            part(middle, 0, 2) + before,
            part(middle, 2, length - 2),
            part(middle, length - 2, length) + after,
        ]
    else:
        pieces = [
            part(before, 0, width - 1),
            part(middle, 0, 2) + part(before, width - 1, width + 1),
            part(middle, 2, length - 2),
            part(middle, length - 2, length) + part(after, 0, 2),
            part(after, 2, width + 1),
        ]
    return jnp.concatenate(pieces, axis=dim)


def spread_kernel(width, ghosts, out, z_out, z_in, mid, x_in, y_out, y_in, send_sems, recv_sems):
    _, size_x, size_y, size_z = ghosts.shape
    layers = width + 1
    greet()
    z_out[0] = jnp.concatenate([ghosts[d, :, :, size_z - layers :] for d in range(3)], axis=-1)
    z_out[1] = jnp.concatenate([ghosts[d, :, :, :layers] for d in range(3)], axis=-1)
    swap("gz", (z_out.at[0], z_out.at[1]), (z_in.at[0], z_in.at[1]), send_sems, recv_sems)
    for d in range(3):
        cut = slice(d * layers, (d + 1) * layers)
        mid[d] = add_ends(ghosts[d], z_in[0, :, :, cut], z_in[1, :, :, cut], 2, width)
    swap(
        "gx",
        (mid.at[:, pl.ds(size_x - layers, layers)], mid.at[:, pl.ds(0, layers)]),
        (x_in.at[0], x_in.at[1]),
        send_sems,
        recv_sems,
    )
    summed = add_ends(mid[...], x_in[0], x_in[1], 1, width)
    y_out[0] = summed[:, :, size_y - layers :, :]
    y_out[1] = summed[:, :, :layers, :]
    swap("gy", (y_out.at[0], y_out.at[1]), (y_in.at[0], y_in.at[1]), send_sems, recv_sems)
    out[...] = add_ends(summed, y_in[0], y_in[1], 2, width)


def spread_sums(ghosts, width):
    _, size_x, size_y, size_z = ghosts.shape
    more = 2 * (width - 1)
    z_slab = (2, size_x, size_y, 3 * (width + 1))
    x_slab = (2, 3, width + 1, size_y, size_z + more)
    y_slab = (2, 3, size_x + more, width + 1, size_z + more)
    return call_kernel(
        functools.partial(spread_kernel, width),
        ghosts,
        (3, size_x + more, size_y + more, size_z + more),
        [z_slab, z_slab, (3, size_x, size_y, size_z + more), x_slab, y_slab, y_slab],
        width,
    )


def project(vector, direction):
    summed = None
    for d in range(3):
        if direction[d] != 0:
            signed = vector[d] if direction[d] > 0 else -vector[d]
            summed = signed if summed is None else summed + signed
    return summed


def moments(fields):
    density = fields[0]
    for i in range(1, 19):
        density = density + fields[i]
    components = []
    for d in range(3):
        summed = None
        for i in range(1, 19):
            if directions[i][d] != 0:
                signed = fields[i] if directions[i][d] > 0 else -fields[i]
                summed = signed if summed is None else summed + signed
        components.append(summed)
    return (density, jnp.stack(components))


def collide(fields, density, velocity, cell_force, gray_fraction):
    flow_square = velocity[0] * velocity[0] + velocity[1] * velocity[1] + velocity[2] * velocity[2]
    post_list = []
    for i in range(19):
        baseline = density - 1.5 * flow_square
        if i > 0:
            along_flow = project(velocity, directions[i])
            along_force = project(cell_force, directions[i])
            baseline = baseline + 3.0 * along_flow + 4.5 * along_flow * along_flow
        equilibrium = weights[i] * baseline
        relaxed = fields[i] + relax_rate * (equilibrium - fields[i])
        if i > 0:
            relaxed = relaxed + 3.0 * weights[i] * along_force
        post_list.append((1.0 - gray_fraction) * relaxed + gray_fraction * fields[opposite[i]])
    return post_list


def propagate(post_list):
    moved = []
    for i in range(19):
        layer = post_list[i]
        for dim in range(3):
            start = 1 - directions[i][dim]
            layer = lax.slice_in_dim(layer, start, start + layer.shape[dim] - 2, axis=dim)
        moved.append(layer)
    return moved


def per_device(
    populations,
    solid_class,
    part_offset,
    part_velocity,
    part_drag,
    part_cell,
    block_rows,
    block_dest,
):
    size_x, size_y, size_z = (populations.shape[1], populations.shape[2], populations.shape[3])
    rows_block = part_cell.shape[1]
    block_count = block_dest.shape[0]
    peers = lax.axis_size("gx")
    capacity = 2 * block_count // peers
    slot_count = peers * capacity
    destination = block_dest[:, 0]
    onehot = (destination[:, None] == jnp.arange(peers, dtype=jnp.int32)[None, :]).astype(jnp.int32)
    before = jnp.cumsum(onehot, axis=0) - onehot
    block_rank = jnp.sum(before * onehot, axis=1)
    slot_index = destination * capacity + block_rank
    match = slot_index[None, :] == jnp.arange(slot_count, dtype=jnp.int32)[:, None]
    filled = jnp.any(match, axis=1)
    source = jnp.sum(jnp.where(match, jnp.arange(block_count, dtype=jnp.int32)[None, :], 0), axis=1)
    alive = jnp.arange(rows_block, dtype=jnp.int32)[None, :] < block_rows[:, None]
    named = jnp.where(alive, part_cell, -1).astype(jnp.float32)
    floats = jnp.concatenate(
        [part_offset, part_velocity, part_drag[:, None, :], named[:, None, :]], axis=1
    )
    empty = jnp.where(jnp.arange(8) == 7, -1.0, 0.0).astype(jnp.float32)[None, :, None]
    send_floats = jnp.where(filled[:, None, None], jnp.take(floats, source, axis=0), empty)
    got_floats = lax.all_to_all(send_floats, "gx", split_axis=0, concat_axis=0, tiled=True)
    offset = got_floats[:, 0:3, :]
    velocity = got_floats[:, 3:6, :]
    drag_rate = got_floats[:, 6, :]
    live_rows = got_floats[:, 7, :] >= 0.0
    got_cells = jnp.maximum(got_floats[:, 7, :], 0.0).astype(jnp.int32)
    p = got_cells // (size_y * size_z) + 1
    q = got_cells // size_z % size_y + 1
    s = got_cells % size_z + 1
    slots = offset.shape[0]
    tables = []
    for d, (place, extent) in enumerate(((p, size_x + 2), (q, size_y + 2), (s, size_z + 2))):
        displace = offset[:, d, :].reshape(-1)
        nearer = place.reshape(-1)
        farther = nearer + jnp.where(displace >= 0.0, 1, -1).astype(jnp.int32)
        grid = jnp.arange(extent, dtype=jnp.int32)[None, :]
        tables.append(
            jnp.where(grid == nearer[:, None], (1.0 - jnp.abs(displace))[:, None], 0.0)
            + jnp.where(grid == farther[:, None], jnp.abs(displace)[:, None], 0.0)
        )
    across = (tables[0][:, :, None] * tables[1][:, None, :]).reshape(slots * rows_block, -1)
    gray = solid_class.astype(jnp.float32) * 0.25
    wide = with_halo(jnp.concatenate([populations, gray[None]]), STEPS)
    fields = [wide[i] for i in range(19)]
    gray_fraction = wide[19]
    for repeat in range(STEPS):
        reach = STEPS - repeat
        density, flow = moments(fields)
        near = flow
        for d, size in enumerate((size_x, size_y, size_z)):
            near = lax.slice_in_dim(near, reach - 1, reach + 1 + size, axis=d + 1)
        lines = near.reshape(3, -1, size_z + 2)
        along = jnp.einsum("nz,dkz->dnk", tables[2], lines, precision=lax.Precision.HIGH)
        sampled = jnp.sum(along * across[None], axis=2).reshape(3, slots, rows_block)
        sampled = jnp.moveaxis(sampled, 0, 1)
        drag_force = jnp.where(
            live_rows[:, None, :], drag_rate[:, None, :] * (sampled - velocity), 0.0
        )
        velocity = velocity + drag_force
        pushed = -jnp.moveaxis(drag_force, 1, 0).reshape(3, -1)
        ghosts = jnp.einsum(
            "dnk,nz->dkz", pushed[:, :, None] * across[None], tables[2],
            precision=lax.Precision.HIGH,
        )
        ghosts = ghosts.reshape(3, size_x + 2, size_y + 2, size_z + 2)
        cell_force = spread_sums(ghosts, reach)
        post_list = collide(fields, density, flow, cell_force, gray_fraction)
        fields = propagate(post_list)
        gray_fraction = gray_fraction[1:-1, 1:-1, 1:-1]
    density, flow = moments(fields)
    fluid_velocity = flow / speed_unit
    particle_velocity = jnp.where(live_rows[:, None, :], velocity / speed_unit, 0.0)
    return (fluid_velocity, particle_velocity)


def solution(mesh):
    in_specs = (
        P(None, "gx", "gy", "gz"),
        P("gx", "gy", "gz"),
        P(("gx", "gy", "gz"), None, None),
        P(("gx", "gy", "gz"), None, None),
        P(("gx", "gy", "gz"), None),
        P(("gx", "gy", "gz"), None),
        P(("gx", "gy", "gz")),
        P(("gx", "gy", "gz"), None),
    )
    out_specs = (P(None, "gx", "gy", "gz"), P(("gx", "gy", "gz"), None, None))
    return jax.shard_map(
        per_device, mesh=mesh, in_specs=in_specs, out_specs=out_specs, check_vma=False
    )
```

```python
import functools

import jax
import jax.numpy as jnp
from jax import lax
from jax.experimental import pallas as pl
from jax.experimental.pallas import tpu as pltpu
from jax.sharding import PartitionSpec as P

STEPS = 2


directions = (
    (0, 0, 0),
    (1, 0, 0),
    (-1, 0, 0),
    (0, 1, 0),
    (0, -1, 0),
    (0, 0, 1),
    (0, 0, -1),
    (1, 1, 0),
    (-1, -1, 0),
    (1, -1, 0),
    (-1, 1, 0),
    (1, 0, 1),
    (-1, 0, -1),
    (1, 0, -1),
    (-1, 0, 1),
    (0, 1, 1),
    (0, -1, -1),
    (0, 1, -1),
    (0, -1, 1),
)
weights = (1.0 / 3.0,) + (1.0 / 18.0,) * 6 + (1.0 / 36.0,) * 12
opposite = (0, 2, 1, 4, 3, 6, 5, 8, 7, 10, 9, 12, 11, 14, 13, 16, 15, 18, 17)
relax_rate = 1.25
speed_unit = 0.05


AXES = ("gx", "gy", "gz")
MESH = pl.DeviceIdType.MESH


def neighbour(axis, step):
    place = [lax.axis_index(name) for name in AXES]
    count = lax.axis_size(axis)
    where = AXES.index(axis)
    place[where] = lax.rem(place[where] + count + step, count)
    return tuple(place)


def greet():
    barrier = pltpu.get_barrier_semaphore()
    for axis in AXES:
        for step in (1, -1):
            pl.semaphore_signal(barrier, inc=1, device_id=neighbour(axis, step), device_id_type=MESH)
    pl.semaphore_wait(barrier, 6)


def send(axis, sources, targets, send_sems, recv_sems, offset=0):
    copies = []
    for k, step in enumerate((1, -1)):
        number = 2 * AXES.index(axis) + k + offset
        copy = pltpu.make_async_remote_copy(
            src_ref=sources[k],
            dst_ref=targets[k],
            send_sem=send_sems.at[number],
            recv_sem=recv_sems.at[number],
            device_id=neighbour(axis, step),
            device_id_type=MESH,
        )
        copy.start()
        copies.append(copy)
    return copies


def swap(axis, sources, targets, send_sems, recv_sems, offset=0):
    for copy in send(axis, sources, targets, send_sems, recv_sems, offset):
        copy.wait()


def stack_rows(cells, groups):
    per = cells.shape[0] // groups
    return jnp.concatenate([cells[g * per : (g + 1) * per] for g in range(groups)], axis=2)


def part_rows(packed, groups, width):
    return jnp.concatenate(
        [packed[:, :, g * width : (g + 1) * width] for g in range(groups)], axis=0
    )


def widen_kernel(
    width, groups, cells, out, x_in, y_out, y_in, e_out, e_in, mid, z_out, z_in,
    send_sems, recv_sems,
):
    fields, size_x, size_y, size_z = cells.shape
    greet()
    x_copies = send(
        "gx",
        (cells.at[:, pl.ds(size_x - width, width)], cells.at[:, pl.ds(0, width)]),
        (x_in.at[0], x_in.at[1]),
        send_sems,
        recv_sems,
    )
    y_out[0] = stack_rows(cells[:, :, size_y - width :, :], groups)
    y_out[1] = stack_rows(cells[:, :, :width, :], groups)
    y_copies = send("gy", (y_out.at[0], y_out.at[1]), (y_in.at[0], y_in.at[1]), send_sems, recv_sems)
    for copy in x_copies:
        copy.wait()
    for k in range(2):
        e_out[0, :, k * width : (k + 1) * width] = stack_rows(x_in[k, :, :, size_y - width :, :], groups)
        e_out[1, :, k * width : (k + 1) * width] = stack_rows(x_in[k, :, :, :width, :], groups)
    e_copies = send(
        "gy", (e_out.at[0], e_out.at[1]), (e_in.at[0], e_in.at[1]), send_sems, recv_sems, 4
    )
    for copy in y_copies:
        copy.wait()
    mid[:, width : width + size_x] = jnp.concatenate(
        [part_rows(y_in[0], groups, width), cells[...], part_rows(y_in[1], groups, width)], axis=2
    )
    for copy in e_copies:
        copy.wait()
    for k, start in ((0, 0), (1, width + size_x)):
        rows = slice(k * width, (k + 1) * width)
        mid[:, start : start + width] = jnp.concatenate(
            [
                part_rows(e_in[0, :, rows], groups, width),
                x_in[k],
                part_rows(e_in[1, :, rows], groups, width),
            ],
            axis=2,
        )
    z_out[0] = jnp.concatenate([mid[c, :, :, size_z - width :] for c in range(fields)], axis=-1)
    z_out[1] = jnp.concatenate([mid[c, :, :, :width] for c in range(fields)], axis=-1)
    swap("gz", (z_out.at[0], z_out.at[1]), (z_in.at[0], z_in.at[1]), send_sems, recv_sems)
    for c in range(fields):
        cut = slice(c * width, (c + 1) * width)
        out[c] = jnp.concatenate([z_in[0, :, :, cut], mid[c], z_in[1, :, :, cut]], axis=-1)


def call_kernel(kernel, operand, out_shape, scratch, number):
    return pl.pallas_call(
        kernel,
        out_shape=jax.ShapeDtypeStruct(out_shape, jnp.float32),
        in_specs=[pl.BlockSpec(memory_space=pltpu.VMEM)],
        out_specs=pl.BlockSpec(memory_space=pltpu.VMEM),
        scratch_shapes=[pltpu.VMEM(shape, jnp.float32) for shape in scratch]
        + [pltpu.SemaphoreType.DMA((8,)), pltpu.SemaphoreType.DMA((8,))],
        compiler_params=pltpu.CompilerParams(
            collective_id=number, has_side_effects=True, vmem_limit_bytes=40 * 1024 * 1024
        ),
    )(operand)


def with_halo(cells, width):
    fields, size_x, size_y, size_z = cells.shape
    wide_x, wide_y, wide_z = (size_x + 2 * width, size_y + 2 * width, size_z + 2 * width)
    groups = 4 if fields % 4 == 0 else 1
    x_slab = (2, fields, width, size_y, size_z)
    y_slab = (2, fields // groups, size_x, groups * width, size_z)
    e_slab = (2, fields // groups, 2 * width, groups * width, size_z)
    z_slab = (2, wide_x, wide_y, fields * width)
    return call_kernel(
        functools.partial(widen_kernel, width, groups),
        cells,
        (fields, wide_x, wide_y, wide_z),
        [x_slab, y_slab, y_slab, e_slab, e_slab, (fields, wide_x, wide_y, size_z), z_slab, z_slab],
        0,
    )


def pack(slab, lanes):
    planes = [slab[d, k] for d in range(slab.shape[0]) for k in range(slab.shape[1])]
    rest = [plane[:, lanes:] for plane in planes]
    free = lanes - len(planes) * rest[0].shape[1]
    rest.append(jnp.zeros((planes[0].shape[0], free), jnp.float32))
    return jnp.concatenate(
        [plane[:, :lanes] for plane in planes] + [jnp.concatenate(rest, axis=1)], axis=0
    )


def unpack(packed, shape, lanes):
    outer, inner, rows, width = shape
    extra, total = width - lanes, outer * inner
    rest = packed[total * rows :]
    planes = [
        jnp.concatenate(
            [packed[i * rows : (i + 1) * rows], rest[:, i * extra : (i + 1) * extra]], axis=1
        )
        for i in range(total)
    ]
    return jnp.stack([jnp.stack(planes[d * inner : (d + 1) * inner]) for d in range(outer)])


def add_ends(middle, before, after, dim, width):
    length = middle.shape[dim]
    part = functools.partial(lax.slice_in_dim, axis=dim)
    if width == 1:
        pieces = [
            part(middle, 0, 2) + before,
            part(middle, 2, length - 2),
            part(middle, length - 2, length) + after,
        ]
    else:
        pieces = [
            part(before, 0, width - 1),
            part(middle, 0, 2) + part(before, width - 1, width + 1),
            part(middle, 2, length - 2),
            part(middle, length - 2, length) + part(after, 0, 2),
            part(after, 2, width + 1),
        ]
    return jnp.concatenate(pieces, axis=dim)


def spread_kernel(
    width, ghosts, out, z_out, z_in, x_out, x_in, y_out, y_in, send_sems, recv_sems
):
    _, size_x, size_y, size_z = ghosts.shape
    layers, lanes = width + 1, size_z - 2
    greet()
    z_out[0] = jnp.concatenate([ghosts[d, :, :, size_z - layers :] for d in range(3)], axis=-1)
    z_out[1] = jnp.concatenate([ghosts[d, :, :, :layers] for d in range(3)], axis=-1)
    swap("gz", (z_out.at[0], z_out.at[1]), (z_in.at[0], z_in.at[1]), send_sems, recv_sems)
    parts = []
    for d in range(3):
        cut = slice(d * layers, (d + 1) * layers)
        parts.append(add_ends(ghosts[d], z_in[0, :, :, cut], z_in[1, :, :, cut], 2, width))
    summed = jnp.stack(parts)
    x_out[0] = pack(summed[:, size_x - layers :], lanes)
    x_out[1] = pack(summed[:, :layers], lanes)
    swap("gx", (x_out.at[0], x_out.at[1]), (x_in.at[0], x_in.at[1]), send_sems, recv_sems)
    shape = (3, layers, size_y, summed.shape[3])
    summed = add_ends(
        summed, unpack(x_in[0], shape, lanes), unpack(x_in[1], shape, lanes), 1, width
    )
    y_out[0] = pack(summed[:, :, size_y - layers :, :], lanes)
    y_out[1] = pack(summed[:, :, :layers, :], lanes)
    swap("gy", (y_out.at[0], y_out.at[1]), (y_in.at[0], y_in.at[1]), send_sems, recv_sems)
    shape = (3, summed.shape[1], layers, summed.shape[3])
    out[...] = add_ends(
        summed, unpack(y_in[0], shape, lanes), unpack(y_in[1], shape, lanes), 2, width
    )


def spread_sums(ghosts, width):
    _, size_x, size_y, size_z = ghosts.shape
    more = 2 * (width - 1)
    z_slab = (2, size_x, size_y, 3 * (width + 1))
    x_slab = (2, (3 * (width + 1) + 1) * size_y, size_z - 2)
    y_slab = (2, (3 * (size_x + more) + 1) * (width + 1), size_z - 2)
    return call_kernel(
        functools.partial(spread_kernel, width),
        ghosts,
        (3, size_x + more, size_y + more, size_z + more),
        [z_slab, z_slab, x_slab, x_slab, y_slab, y_slab],
        width,
    )


def project(vector, direction):
    summed = None
    for d in range(3):
        if direction[d] != 0:
            signed = vector[d] if direction[d] > 0 else -vector[d]
            summed = signed if summed is None else summed + signed
    return summed


def moments(fields):
    density = fields[0]
    for i in range(1, 19):
        density = density + fields[i]
    components = []
    for d in range(3):
        summed = None
        for i in range(1, 19):
            if directions[i][d] != 0:
                signed = fields[i] if directions[i][d] > 0 else -fields[i]
                summed = signed if summed is None else summed + signed
        components.append(summed)
    return (density, jnp.stack(components))


def collide(fields, density, velocity, cell_force, gray_fraction):
    flow_square = velocity[0] * velocity[0] + velocity[1] * velocity[1] + velocity[2] * velocity[2]
    post_list = []
    for i in range(19):
        baseline = density - 1.5 * flow_square
        if i > 0:
            along_flow = project(velocity, directions[i])
            along_force = project(cell_force, directions[i])
            baseline = baseline + 3.0 * along_flow + 4.5 * along_flow * along_flow
        equilibrium = weights[i] * baseline
        relaxed = fields[i] + relax_rate * (equilibrium - fields[i])
        if i > 0:
            relaxed = relaxed + 3.0 * weights[i] * along_force
        post_list.append((1.0 - gray_fraction) * relaxed + gray_fraction * fields[opposite[i]])
    return post_list


def propagate(post_list):
    moved = []
    for i in range(19):
        layer = post_list[i]
        for dim in range(3):
            start = 1 - directions[i][dim]
            layer = lax.slice_in_dim(layer, start, start + layer.shape[dim] - 2, axis=dim)
        moved.append(layer)
    return moved


def per_device(
    populations,
    solid_class,
    part_offset,
    part_velocity,
    part_drag,
    part_cell,
    block_rows,
    block_dest,
):
    size_x, size_y, size_z = (populations.shape[1], populations.shape[2], populations.shape[3])
    rows_block = part_cell.shape[1]
    block_count = block_dest.shape[0]
    peers = lax.axis_size("gx")
    capacity = 2 * block_count // peers
    slot_count = peers * capacity
    destination = block_dest[:, 0]
    onehot = (destination[:, None] == jnp.arange(peers, dtype=jnp.int32)[None, :]).astype(jnp.int32)
    before = jnp.cumsum(onehot, axis=0) - onehot
    block_rank = jnp.sum(before * onehot, axis=1)
    slot_index = destination * capacity + block_rank
    match = slot_index[None, :] == jnp.arange(slot_count, dtype=jnp.int32)[:, None]
    filled = jnp.any(match, axis=1)
    source = jnp.sum(jnp.where(match, jnp.arange(block_count, dtype=jnp.int32)[None, :], 0), axis=1)
    alive = jnp.arange(rows_block, dtype=jnp.int32)[None, :] < block_rows[:, None]
    named = jnp.where(alive, part_cell, -1).astype(jnp.float32)
    floats = jnp.concatenate(
        [part_offset, part_velocity, part_drag[:, None, :], named[:, None, :]], axis=1
    )
    empty = jnp.where(jnp.arange(8) == 7, -1.0, 0.0).astype(jnp.float32)[None, :, None]
    send_floats = jnp.where(filled[:, None, None], jnp.take(floats, source, axis=0), empty)
    got_floats = lax.all_to_all(send_floats, "gx", split_axis=0, concat_axis=0, tiled=True)
    offset = got_floats[:, 0:3, :]
    velocity = got_floats[:, 3:6, :]
    drag_rate = got_floats[:, 6, :]
    live_rows = got_floats[:, 7, :] >= 0.0
    got_cells = jnp.maximum(got_floats[:, 7, :], 0.0).astype(jnp.int32)
    p = got_cells // (size_y * size_z) + 1
    q = got_cells // size_z % size_y + 1
    s = got_cells % size_z + 1
    slots = offset.shape[0]
    tables = []
    for d, (place, extent) in enumerate(((p, size_x + 2), (q, size_y + 2), (s, size_z + 2))):
        displace = offset[:, d, :].reshape(-1)
        nearer = place.reshape(-1)
        farther = nearer + jnp.where(displace >= 0.0, 1, -1).astype(jnp.int32)
        grid = jnp.arange(extent, dtype=jnp.int32)[None, :]
        tables.append(
            jnp.where(grid == nearer[:, None], (1.0 - jnp.abs(displace))[:, None], 0.0)
            + jnp.where(grid == farther[:, None], jnp.abs(displace)[:, None], 0.0)
        )
    across = (tables[0][:, :, None] * tables[1][:, None, :]).reshape(slots * rows_block, -1)
    gray = solid_class.astype(jnp.float32) * 0.25
    wide = with_halo(jnp.concatenate([populations, gray[None]]), STEPS)
    fields = [wide[i] for i in range(19)]
    gray_fraction = wide[19]
    for repeat in range(STEPS):
        reach = STEPS - repeat
        density, flow = moments(fields)
        near = flow
        for d, size in enumerate((size_x, size_y, size_z)):
            near = lax.slice_in_dim(near, reach - 1, reach + 1 + size, axis=d + 1)
        lines = near.reshape(3, -1, size_z + 2)
        along = jnp.einsum("nz,dkz->dnk", tables[2], lines, precision=lax.Precision.HIGH)
        sampled = jnp.sum(along * across[None], axis=2).reshape(3, slots, rows_block)
        sampled = jnp.moveaxis(sampled, 0, 1)
        drag_force = jnp.where(
            live_rows[:, None, :], drag_rate[:, None, :] * (sampled - velocity), 0.0
        )
        velocity = velocity + drag_force
        pushed = -jnp.moveaxis(drag_force, 1, 0).reshape(3, -1)
        ghosts = jnp.einsum(
            "dnk,nz->dkz", pushed[:, :, None] * across[None], tables[2],
            precision=lax.Precision.HIGH,
        )
        ghosts = ghosts.reshape(3, size_x + 2, size_y + 2, size_z + 2)
        cell_force = spread_sums(ghosts, reach)
        post_list = collide(fields, density, flow, cell_force, gray_fraction)
        fields = propagate(post_list)
        gray_fraction = gray_fraction[1:-1, 1:-1, 1:-1]
    density, flow = moments(fields)
    fluid_velocity = flow / speed_unit
    particle_velocity = jnp.where(live_rows[:, None, :], velocity / speed_unit, 0.0)
    return (fluid_velocity, particle_velocity)


def solution(mesh):
    in_specs = (
        P(None, "gx", "gy", "gz"),
        P("gx", "gy", "gz"),
        P(("gx", "gy", "gz"), None, None),
        P(("gx", "gy", "gz"), None, None),
        P(("gx", "gy", "gz"), None),
        P(("gx", "gy", "gz"), None),
        P(("gx", "gy", "gz")),
        P(("gx", "gy", "gz"), None),
    )
    out_specs = (P(None, "gx", "gy", "gz"), P(("gx", "gy", "gz"), None, None))
    return jax.shard_map(
        per_device, mesh=mesh, in_specs=in_specs, out_specs=out_specs, check_vma=False
    )
```

```python
import functools

import jax
import jax.numpy as jnp
from jax import lax
from jax.experimental import pallas as pl
from jax.experimental.pallas import tpu as pltpu
from jax.sharding import PartitionSpec as P

STEPS = 2


directions = (
    (0, 0, 0),
    (1, 0, 0),
    (-1, 0, 0),
    (0, 1, 0),
    (0, -1, 0),
    (0, 0, 1),
    (0, 0, -1),
    (1, 1, 0),
    (-1, -1, 0),
    (1, -1, 0),
    (-1, 1, 0),
    (1, 0, 1),
    (-1, 0, -1),
    (1, 0, -1),
    (-1, 0, 1),
    (0, 1, 1),
    (0, -1, -1),
    (0, 1, -1),
    (0, -1, 1),
)
weights = (1.0 / 3.0,) + (1.0 / 18.0,) * 6 + (1.0 / 36.0,) * 12
opposite = (0, 2, 1, 4, 3, 6, 5, 8, 7, 10, 9, 12, 11, 14, 13, 16, 15, 18, 17)
relax_rate = 1.25
speed_unit = 0.05


AXES = ("gx", "gy", "gz")
MESH = pl.DeviceIdType.MESH


def neighbour(axis, step):
    place = [lax.axis_index(name) for name in AXES]
    count = lax.axis_size(axis)
    where = AXES.index(axis)
    place[where] = lax.rem(place[where] + count + step, count)
    return tuple(place)


def greet(peers=1):
    barrier = pltpu.get_barrier_semaphore()
    for step in range(1, peers):
        pl.semaphore_signal(barrier, inc=1, device_id=neighbour("gx", step), device_id_type=MESH)
    for axis in AXES:
        for step in (1, -1):
            pl.semaphore_signal(barrier, inc=1, device_id=neighbour(axis, step), device_id_type=MESH)
    pl.semaphore_wait(barrier, 5 + peers)


def send(axis, sources, targets, send_sems, recv_sems, offset=0):
    copies = []
    for k, step in enumerate((1, -1)):
        number = 2 * AXES.index(axis) + k + offset
        copy = pltpu.make_async_remote_copy(
            src_ref=sources[k],
            dst_ref=targets[k],
            send_sem=send_sems.at[number],
            recv_sem=recv_sems.at[number],
            device_id=neighbour(axis, step),
            device_id_type=MESH,
        )
        copy.start()
        copies.append(copy)
    return copies


def swap(axis, sources, targets, send_sems, recv_sems, offset=0):
    for copy in send(axis, sources, targets, send_sems, recv_sems, offset):
        copy.wait()


def stack_rows(cells, groups):
    per = cells.shape[0] // groups
    return jnp.concatenate([cells[g * per : (g + 1) * per] for g in range(groups)], axis=2)


def part_rows(packed, groups, width):
    return jnp.concatenate(
        [packed[:, :, g * width : (g + 1) * width] for g in range(groups)], axis=0
    )


def widen_kernel(
    width, groups, peers, cells, blocks, out, got, x_in, y_out, y_in, e_out, e_in, mid, z_out,
    z_in, arrived, send_sems, recv_sems, give_sems, take_sems,
):
    fields, size_x, size_y, size_z = cells.shape
    capacity = blocks.shape[0] // peers
    me = lax.axis_index("gx")
    greet(peers)
    x_copies = send(
        "gx",
        (cells.at[:, pl.ds(size_x - width, width)], cells.at[:, pl.ds(0, width)]),
        (x_in.at[0], x_in.at[1]),
        send_sems,
        recv_sems,
    )
    block_copies = []
    for step in range(1, peers):
        copy = pltpu.make_async_remote_copy(
            src_ref=blocks.at[pl.ds(lax.rem(me + step, peers) * capacity, capacity)],
            dst_ref=arrived.at[pl.ds(me * capacity, capacity)],
            send_sem=give_sems.at[step - 1],
            recv_sem=take_sems.at[step - 1],
            device_id=neighbour("gx", step),
            device_id_type=MESH,
        )
        copy.start()
        block_copies.append(copy)
    arrived[pl.ds(me * capacity, capacity)] = blocks[pl.ds(me * capacity, capacity)]
    y_out[0] = stack_rows(cells[:, :, size_y - width :, :], groups)
    y_out[1] = stack_rows(cells[:, :, :width, :], groups)
    y_copies = send("gy", (y_out.at[0], y_out.at[1]), (y_in.at[0], y_in.at[1]), send_sems, recv_sems)
    for copy in x_copies:
        copy.wait()
    for k in range(2):
        e_out[0, :, k * width : (k + 1) * width] = stack_rows(x_in[k, :, :, size_y - width :, :], groups)
        e_out[1, :, k * width : (k + 1) * width] = stack_rows(x_in[k, :, :, :width, :], groups)
    e_copies = send(
        "gy", (e_out.at[0], e_out.at[1]), (e_in.at[0], e_in.at[1]), send_sems, recv_sems, 4
    )
    for copy in y_copies:
        copy.wait()
    mid[:, width : width + size_x] = jnp.concatenate(
        [part_rows(y_in[0], groups, width), cells[...], part_rows(y_in[1], groups, width)], axis=2
    )
    for copy in e_copies:
        copy.wait()
    for k, start in ((0, 0), (1, width + size_x)):
        rows = slice(k * width, (k + 1) * width)
        mid[:, start : start + width] = jnp.concatenate(
            [
                part_rows(e_in[0, :, rows], groups, width),
                x_in[k],
                part_rows(e_in[1, :, rows], groups, width),
            ],
            axis=2,
        )
    z_out[0] = jnp.concatenate([mid[c, :, :, size_z - width :] for c in range(fields)], axis=-1)
    z_out[1] = jnp.concatenate([mid[c, :, :, :width] for c in range(fields)], axis=-1)
    swap("gz", (z_out.at[0], z_out.at[1]), (z_in.at[0], z_in.at[1]), send_sems, recv_sems)
    for c in range(fields):
        cut = slice(c * width, (c + 1) * width)
        out[c] = jnp.concatenate([z_in[0, :, :, cut], mid[c], z_in[1, :, :, cut]], axis=-1)
    for copy in block_copies:
        copy.wait()
    got[...] = arrived[...]


def call_kernel(kernel, operands, out_shapes, scratch, number, peers=1):
    vmem = pl.BlockSpec(memory_space=pltpu.VMEM)
    counts = (8, 8) + ((peers - 1,) * 2 if peers > 1 else ())
    return pl.pallas_call(
        kernel,
        out_shape=[jax.ShapeDtypeStruct(shape, jnp.float32) for shape in out_shapes],
        in_specs=[vmem for _ in operands],
        out_specs=[vmem for _ in out_shapes],
        scratch_shapes=[pltpu.VMEM(shape, jnp.float32) for shape in scratch]
        + [pltpu.SemaphoreType.DMA((count,)) for count in counts],
        compiler_params=pltpu.CompilerParams(
            collective_id=number, has_side_effects=True, vmem_limit_bytes=40 * 1024 * 1024
        ),
    )(*operands)


def with_halo(cells, blocks, peers, width):
    fields, size_x, size_y, size_z = cells.shape
    wide_x, wide_y, wide_z = (size_x + 2 * width, size_y + 2 * width, size_z + 2 * width)
    groups = 4 if fields % 4 == 0 else 1
    x_slab = (2, fields, width, size_y, size_z)
    y_slab = (2, fields // groups, size_x, groups * width, size_z)
    e_slab = (2, fields // groups, 2 * width, groups * width, size_z)
    z_slab = (2, wide_x, wide_y, fields * width)
    return call_kernel(
        functools.partial(widen_kernel, width, groups, peers),
        (cells, blocks),
        ((fields, wide_x, wide_y, wide_z), blocks.shape),
        [x_slab, y_slab, y_slab, e_slab, e_slab, (fields, wide_x, wide_y, size_z), z_slab, z_slab]
        + [blocks.shape],
        0,
        peers,
    )


def pack(slab, lanes):
    planes = [slab[d, k] for d in range(slab.shape[0]) for k in range(slab.shape[1])]
    rest = [plane[:, lanes:] for plane in planes]
    free = lanes - len(planes) * rest[0].shape[1]
    rest.append(jnp.zeros((planes[0].shape[0], free), jnp.float32))
    return jnp.concatenate(
        [plane[:, :lanes] for plane in planes] + [jnp.concatenate(rest, axis=1)], axis=0
    )


def unpack(packed, shape, lanes):
    outer, inner, rows, width = shape
    extra, total = width - lanes, outer * inner
    rest = packed[total * rows :]
    planes = [
        jnp.concatenate(
            [packed[i * rows : (i + 1) * rows], rest[:, i * extra : (i + 1) * extra]], axis=1
        )
        for i in range(total)
    ]
    return jnp.stack([jnp.stack(planes[d * inner : (d + 1) * inner]) for d in range(outer)])


def add_ends(middle, before, after, dim, width):
    length = middle.shape[dim]
    part = functools.partial(lax.slice_in_dim, axis=dim)
    if width == 1:
        pieces = [
            part(middle, 0, 2) + before,
            part(middle, 2, length - 2),
            part(middle, length - 2, length) + after,
        ]
    else:
        pieces = [
            part(before, 0, width - 1),
            part(middle, 0, 2) + part(before, width - 1, width + 1),
            part(middle, 2, length - 2),
            part(middle, length - 2, length) + part(after, 0, 2),
            part(after, 2, width + 1),
        ]
    return jnp.concatenate(pieces, axis=dim)


def spread_kernel(
    width, ghosts, out, z_out, z_in, x_out, x_in, y_out, y_in, send_sems, recv_sems
):
    _, size_x, size_y, size_z = ghosts.shape
    layers, lanes = width + 1, size_z - 2
    greet()
    z_out[0] = jnp.concatenate([ghosts[d, :, :, size_z - layers :] for d in range(3)], axis=-1)
    z_out[1] = jnp.concatenate([ghosts[d, :, :, :layers] for d in range(3)], axis=-1)
    swap("gz", (z_out.at[0], z_out.at[1]), (z_in.at[0], z_in.at[1]), send_sems, recv_sems)
    parts = []
    for d in range(3):
        cut = slice(d * layers, (d + 1) * layers)
        parts.append(add_ends(ghosts[d], z_in[0, :, :, cut], z_in[1, :, :, cut], 2, width))
    summed = jnp.stack(parts)
    x_out[0] = pack(summed[:, size_x - layers :], lanes)
    x_out[1] = pack(summed[:, :layers], lanes)
    swap("gx", (x_out.at[0], x_out.at[1]), (x_in.at[0], x_in.at[1]), send_sems, recv_sems)
    shape = (3, layers, size_y, summed.shape[3])
    summed = add_ends(
        summed, unpack(x_in[0], shape, lanes), unpack(x_in[1], shape, lanes), 1, width
    )
    y_out[0] = pack(summed[:, :, size_y - layers :, :], lanes)
    y_out[1] = pack(summed[:, :, :layers, :], lanes)
    swap("gy", (y_out.at[0], y_out.at[1]), (y_in.at[0], y_in.at[1]), send_sems, recv_sems)
    shape = (3, summed.shape[1], layers, summed.shape[3])
    out[...] = add_ends(
        summed, unpack(y_in[0], shape, lanes), unpack(y_in[1], shape, lanes), 2, width
    )


def spread_sums(ghosts, width):
    _, size_x, size_y, size_z = ghosts.shape
    more = 2 * (width - 1)
    z_slab = (2, size_x, size_y, 3 * (width + 1))
    x_slab = (2, (3 * (width + 1) + 1) * size_y, size_z - 2)
    y_slab = (2, (3 * (size_x + more) + 1) * (width + 1), size_z - 2)
    return call_kernel(
        functools.partial(spread_kernel, width),
        (ghosts,),
        ((3, size_x + more, size_y + more, size_z + more),),
        [z_slab, z_slab, x_slab, x_slab, y_slab, y_slab],
        width,
    )[0]


def project(vector, direction):
    summed = None
    for d in range(3):
        if direction[d] != 0:
            signed = vector[d] if direction[d] > 0 else -vector[d]
            summed = signed if summed is None else summed + signed
    return summed


def moments(fields):
    density = fields[0]
    for i in range(1, 19):
        density = density + fields[i]
    components = []
    for d in range(3):
        summed = None
        for i in range(1, 19):
            if directions[i][d] != 0:
                signed = fields[i] if directions[i][d] > 0 else -fields[i]
                summed = signed if summed is None else summed + signed
        components.append(summed)
    return (density, jnp.stack(components))


def collide(fields, density, velocity, cell_force, gray_fraction):
    flow_square = velocity[0] * velocity[0] + velocity[1] * velocity[1] + velocity[2] * velocity[2]
    post_list = []
    for i in range(19):
        baseline = density - 1.5 * flow_square
        if i > 0:
            along_flow = project(velocity, directions[i])
            along_force = project(cell_force, directions[i])
            baseline = baseline + 3.0 * along_flow + 4.5 * along_flow * along_flow
        equilibrium = weights[i] * baseline
        relaxed = fields[i] + relax_rate * (equilibrium - fields[i])
        if i > 0:
            relaxed = relaxed + 3.0 * weights[i] * along_force
        post_list.append((1.0 - gray_fraction) * relaxed + gray_fraction * fields[opposite[i]])
    return post_list


def propagate(post_list):
    moved = []
    for i in range(19):
        layer = post_list[i]
        for dim in range(3):
            start = 1 - directions[i][dim]
            layer = lax.slice_in_dim(layer, start, start + layer.shape[dim] - 2, axis=dim)
        moved.append(layer)
    return moved


def per_device(
    populations,
    solid_class,
    part_offset,
    part_velocity,
    part_drag,
    part_cell,
    block_rows,
    block_dest,
):
    size_x, size_y, size_z = (populations.shape[1], populations.shape[2], populations.shape[3])
    rows_block = part_cell.shape[1]
    block_count = block_dest.shape[0]
    peers = lax.axis_size("gx")
    capacity = 2 * block_count // peers
    slot_count = peers * capacity
    destination = block_dest[:, 0]
    onehot = (destination[:, None] == jnp.arange(peers, dtype=jnp.int32)[None, :]).astype(jnp.int32)
    before = jnp.cumsum(onehot, axis=0) - onehot
    block_rank = jnp.sum(before * onehot, axis=1)
    slot_index = destination * capacity + block_rank
    match = slot_index[None, :] == jnp.arange(slot_count, dtype=jnp.int32)[:, None]
    filled = jnp.any(match, axis=1)
    source = jnp.sum(jnp.where(match, jnp.arange(block_count, dtype=jnp.int32)[None, :], 0), axis=1)
    alive = jnp.arange(rows_block, dtype=jnp.int32)[None, :] < block_rows[:, None]
    named = jnp.where(alive, part_cell, -1).astype(jnp.float32)
    floats = jnp.concatenate(
        [part_offset, part_velocity, part_drag[:, None, :], named[:, None, :]], axis=1
    )
    empty = jnp.where(jnp.arange(8) == 7, -1.0, 0.0).astype(jnp.float32)[None, :, None]
    send_floats = jnp.where(filled[:, None, None], jnp.take(floats, source, axis=0), empty)
    gray = solid_class.astype(jnp.float32) * 0.25
    wide, got_floats = with_halo(
        jnp.concatenate([populations, gray[None]]), send_floats, peers, STEPS
    )
    offset = got_floats[:, 0:3, :]
    velocity = got_floats[:, 3:6, :]
    drag_rate = got_floats[:, 6, :]
    live_rows = got_floats[:, 7, :] >= 0.0
    got_cells = jnp.maximum(got_floats[:, 7, :], 0.0).astype(jnp.int32)
    p = got_cells // (size_y * size_z) + 1
    q = got_cells // size_z % size_y + 1
    s = got_cells % size_z + 1
    slots = offset.shape[0]
    tables = []
    for d, (place, extent) in enumerate(((p, size_x + 2), (q, size_y + 2), (s, size_z + 2))):
        displace = offset[:, d, :].reshape(-1)
        nearer = place.reshape(-1)
        farther = nearer + jnp.where(displace >= 0.0, 1, -1).astype(jnp.int32)
        grid = jnp.arange(extent, dtype=jnp.int32)[None, :]
        tables.append(
            jnp.where(grid == nearer[:, None], (1.0 - jnp.abs(displace))[:, None], 0.0)
            + jnp.where(grid == farther[:, None], jnp.abs(displace)[:, None], 0.0)
        )
    across = (tables[0][:, :, None] * tables[1][:, None, :]).reshape(slots * rows_block, -1)
    fields = [wide[i] for i in range(19)]
    gray_fraction = wide[19]
    for repeat in range(STEPS):
        reach = STEPS - repeat
        density, flow = moments(fields)
        near = flow
        for d, size in enumerate((size_x, size_y, size_z)):
            near = lax.slice_in_dim(near, reach - 1, reach + 1 + size, axis=d + 1)
        lines = near.reshape(3, -1, size_z + 2)
        along = jnp.einsum("nz,dkz->dnk", tables[2], lines, precision=lax.Precision.HIGH)
        sampled = jnp.sum(along * across[None], axis=2).reshape(3, slots, rows_block)
        sampled = jnp.moveaxis(sampled, 0, 1)
        drag_force = jnp.where(
            live_rows[:, None, :], drag_rate[:, None, :] * (sampled - velocity), 0.0
        )
        velocity = velocity + drag_force
        pushed = -jnp.moveaxis(drag_force, 1, 0).reshape(3, -1)
        ghosts = jnp.einsum(
            "dnk,nz->dkz", pushed[:, :, None] * across[None], tables[2],
            precision=lax.Precision.HIGH,
        )
        ghosts = ghosts.reshape(3, size_x + 2, size_y + 2, size_z + 2)
        cell_force = spread_sums(ghosts, reach)
        post_list = collide(fields, density, flow, cell_force, gray_fraction)
        fields = propagate(post_list)
        gray_fraction = gray_fraction[1:-1, 1:-1, 1:-1]
    density, flow = moments(fields)
    fluid_velocity = flow / speed_unit
    particle_velocity = jnp.where(live_rows[:, None, :], velocity / speed_unit, 0.0)
    return (fluid_velocity, particle_velocity)


def solution(mesh):
    in_specs = (
        P(None, "gx", "gy", "gz"),
        P("gx", "gy", "gz"),
        P(("gx", "gy", "gz"), None, None),
        P(("gx", "gy", "gz"), None, None),
        P(("gx", "gy", "gz"), None),
        P(("gx", "gy", "gz"), None),
        P(("gx", "gy", "gz")),
        P(("gx", "gy", "gz"), None),
    )
    out_specs = (P(None, "gx", "gy", "gz"), P(("gx", "gy", "gz"), None, None))
    return jax.shard_map(
        per_device, mesh=mesh, in_specs=in_specs, out_specs=out_specs, check_vma=False
    )
```

```python
import functools

import jax
import jax.numpy as jnp
from jax import lax
from jax.experimental import pallas as pl
from jax.experimental.pallas import tpu as pltpu
from jax.sharding import PartitionSpec as P

STEPS = 2


directions = (
    (0, 0, 0),
    (1, 0, 0),
    (-1, 0, 0),
    (0, 1, 0),
    (0, -1, 0),
    (0, 0, 1),
    (0, 0, -1),
    (1, 1, 0),
    (-1, -1, 0),
    (1, -1, 0),
    (-1, 1, 0),
    (1, 0, 1),
    (-1, 0, -1),
    (1, 0, -1),
    (-1, 0, 1),
    (0, 1, 1),
    (0, -1, -1),
    (0, 1, -1),
    (0, -1, 1),
)
weights = (1.0 / 3.0,) + (1.0 / 18.0,) * 6 + (1.0 / 36.0,) * 12
opposite = (0, 2, 1, 4, 3, 6, 5, 8, 7, 10, 9, 12, 11, 14, 13, 16, 15, 18, 17)
relax_rate = 1.25
speed_unit = 0.05


AXES = ("gx", "gy", "gz")
MESH = pl.DeviceIdType.MESH


def neighbour(axis, step):
    place = [lax.axis_index(name) for name in AXES]
    count = lax.axis_size(axis)
    where = AXES.index(axis)
    place[where] = lax.rem(place[where] + count + step, count)
    return tuple(place)


def greet(peers=1):
    barrier = pltpu.get_barrier_semaphore()
    for step in range(1, peers):
        pl.semaphore_signal(barrier, inc=1, device_id=neighbour("gx", step), device_id_type=MESH)
    for axis in AXES:
        for step in (1, -1):
            pl.semaphore_signal(barrier, inc=1, device_id=neighbour(axis, step), device_id_type=MESH)
    pl.semaphore_wait(barrier, 5 + peers)


def send(axis, sources, targets, send_sems, recv_sems, offset=0):
    copies = []
    for k, step in enumerate((1, -1)):
        number = 2 * AXES.index(axis) + k + offset
        copy = pltpu.make_async_remote_copy(
            src_ref=sources[k],
            dst_ref=targets[k],
            send_sem=send_sems.at[number],
            recv_sem=recv_sems.at[number],
            device_id=neighbour(axis, step),
            device_id_type=MESH,
        )
        copy.start()
        copies.append(copy)
    return copies


def swap(axis, sources, targets, send_sems, recv_sems, offset=0):
    for copy in send(axis, sources, targets, send_sems, recv_sems, offset):
        copy.wait()


def stack_rows(cells, groups):
    per = cells.shape[0] // groups
    return jnp.concatenate([cells[g * per : (g + 1) * per] for g in range(groups)], axis=2)


def part_rows(packed, groups, width):
    return jnp.concatenate(
        [packed[:, :, g * width : (g + 1) * width] for g in range(groups)], axis=0
    )


def widen_kernel(
    width, groups, peers, given, solid, blocks, out, got, cells, x_in, y_out, y_in, e_out, e_in, mid, z_out,
    z_in, arrived, send_sems, recv_sems, give_sems, take_sems,
):
    fields, size_x, size_y, size_z = cells.shape
    capacity = blocks.shape[0] // peers
    me = lax.axis_index("gx")
    cells[: fields - 1] = given[...]
    cells[fields - 1] = solid[...].astype(jnp.float32) * 0.25
    greet(peers)
    x_copies = send(
        "gx",
        (cells.at[:, pl.ds(size_x - width, width)], cells.at[:, pl.ds(0, width)]),
        (x_in.at[0], x_in.at[1]),
        send_sems,
        recv_sems,
    )
    block_copies = []
    for step in range(1, peers):
        copy = pltpu.make_async_remote_copy(
            src_ref=blocks.at[pl.ds(lax.rem(me + step, peers) * capacity, capacity)],
            dst_ref=arrived.at[pl.ds(me * capacity, capacity)],
            send_sem=give_sems.at[step - 1],
            recv_sem=take_sems.at[step - 1],
            device_id=neighbour("gx", step),
            device_id_type=MESH,
        )
        copy.start()
        block_copies.append(copy)
    arrived[pl.ds(me * capacity, capacity)] = blocks[pl.ds(me * capacity, capacity)]
    y_out[0] = stack_rows(cells[:, :, size_y - width :, :], groups)
    y_out[1] = stack_rows(cells[:, :, :width, :], groups)
    y_copies = send("gy", (y_out.at[0], y_out.at[1]), (y_in.at[0], y_in.at[1]), send_sems, recv_sems)
    for copy in x_copies:
        copy.wait()
    for k in range(2):
        e_out[0, :, k * width : (k + 1) * width] = stack_rows(x_in[k, :, :, size_y - width :, :], groups)
        e_out[1, :, k * width : (k + 1) * width] = stack_rows(x_in[k, :, :, :width, :], groups)
    e_copies = send(
        "gy", (e_out.at[0], e_out.at[1]), (e_in.at[0], e_in.at[1]), send_sems, recv_sems, 4
    )
    for copy in y_copies:
        copy.wait()
    mid[:, width : width + size_x] = jnp.concatenate(
        [part_rows(y_in[0], groups, width), cells[...], part_rows(y_in[1], groups, width)], axis=2
    )
    for copy in e_copies:
        copy.wait()
    for k, start in ((0, 0), (1, width + size_x)):
        rows = slice(k * width, (k + 1) * width)
        mid[:, start : start + width] = jnp.concatenate(
            [
                part_rows(e_in[0, :, rows], groups, width),
                x_in[k],
                part_rows(e_in[1, :, rows], groups, width),
            ],
            axis=2,
        )
    z_out[0] = jnp.concatenate([mid[c, :, :, size_z - width :] for c in range(fields)], axis=-1)
    z_out[1] = jnp.concatenate([mid[c, :, :, :width] for c in range(fields)], axis=-1)
    swap("gz", (z_out.at[0], z_out.at[1]), (z_in.at[0], z_in.at[1]), send_sems, recv_sems)
    for c in range(fields):
        cut = slice(c * width, (c + 1) * width)
        out[c] = jnp.concatenate([z_in[0, :, :, cut], mid[c], z_in[1, :, :, cut]], axis=-1)
    for copy in block_copies:
        copy.wait()
    got[...] = arrived[...]


def call_kernel(kernel, operands, out_shapes, scratch, number, peers=1):
    vmem = pl.BlockSpec(memory_space=pltpu.VMEM)
    counts = (8, 8) + ((peers - 1,) * 2 if peers > 1 else ())
    return pl.pallas_call(
        kernel,
        out_shape=[jax.ShapeDtypeStruct(shape, jnp.float32) for shape in out_shapes],
        in_specs=[vmem for _ in operands],
        out_specs=[vmem for _ in out_shapes],
        scratch_shapes=[pltpu.VMEM(shape, jnp.float32) for shape in scratch]
        + [pltpu.SemaphoreType.DMA((count,)) for count in counts],
        compiler_params=pltpu.CompilerParams(
            collective_id=number, has_side_effects=True, vmem_limit_bytes=40 * 1024 * 1024
        ),
    )(*operands)


def with_halo(populations, solid, blocks, peers, width):
    fields, size_x, size_y, size_z = (populations.shape[0] + 1,) + populations.shape[1:]
    wide_x, wide_y, wide_z = (size_x + 2 * width, size_y + 2 * width, size_z + 2 * width)
    groups = 4 if fields % 4 == 0 else 1
    x_slab = (2, fields, width, size_y, size_z)
    y_slab = (2, fields // groups, size_x, groups * width, size_z)
    e_slab = (2, fields // groups, 2 * width, groups * width, size_z)
    z_slab = (2, wide_x, wide_y, fields * width)
    return call_kernel(
        functools.partial(widen_kernel, width, groups, peers),
        (populations, solid, blocks),
        ((fields, wide_x, wide_y, wide_z), blocks.shape),
        [(fields, size_x, size_y, size_z)]
        + [x_slab, y_slab, y_slab, e_slab, e_slab, (fields, wide_x, wide_y, size_z), z_slab, z_slab]
        + [blocks.shape],
        0,
        peers,
    )


def pack(slab, lanes):
    planes = [slab[d, k] for d in range(slab.shape[0]) for k in range(slab.shape[1])]
    rest = [plane[:, lanes:] for plane in planes]
    free = lanes - len(planes) * rest[0].shape[1]
    rest.append(jnp.zeros((planes[0].shape[0], free), jnp.float32))
    return jnp.concatenate(
        [plane[:, :lanes] for plane in planes] + [jnp.concatenate(rest, axis=1)], axis=0
    )


def unpack(packed, shape, lanes):
    outer, inner, rows, width = shape
    extra, total = width - lanes, outer * inner
    rest = packed[total * rows :]
    planes = [
        jnp.concatenate(
            [packed[i * rows : (i + 1) * rows], rest[:, i * extra : (i + 1) * extra]], axis=1
        )
        for i in range(total)
    ]
    return jnp.stack([jnp.stack(planes[d * inner : (d + 1) * inner]) for d in range(outer)])


def add_ends(middle, before, after, dim, width):
    length = middle.shape[dim]
    part = functools.partial(lax.slice_in_dim, axis=dim)
    if width == 1:
        pieces = [
            part(middle, 0, 2) + before,
            part(middle, 2, length - 2),
            part(middle, length - 2, length) + after,
        ]
    else:
        pieces = [
            part(before, 0, width - 1),
            part(middle, 0, 2) + part(before, width - 1, width + 1),
            part(middle, 2, length - 2),
            part(middle, length - 2, length) + part(after, 0, 2),
            part(after, 2, width + 1),
        ]
    return jnp.concatenate(pieces, axis=dim)


def spread_kernel(
    width, ghosts, out, z_out, z_in, x_out, x_in, y_out, y_in, send_sems, recv_sems
):
    _, size_x, size_y, size_z = ghosts.shape
    layers, lanes = width + 1, size_z - 2
    greet()
    z_out[0] = jnp.concatenate([ghosts[d, :, :, size_z - layers :] for d in range(3)], axis=-1)
    z_out[1] = jnp.concatenate([ghosts[d, :, :, :layers] for d in range(3)], axis=-1)
    swap("gz", (z_out.at[0], z_out.at[1]), (z_in.at[0], z_in.at[1]), send_sems, recv_sems)
    parts = []
    for d in range(3):
        cut = slice(d * layers, (d + 1) * layers)
        parts.append(add_ends(ghosts[d], z_in[0, :, :, cut], z_in[1, :, :, cut], 2, width))
    summed = jnp.stack(parts)
    x_out[0] = pack(summed[:, size_x - layers :], lanes)
    x_out[1] = pack(summed[:, :layers], lanes)
    swap("gx", (x_out.at[0], x_out.at[1]), (x_in.at[0], x_in.at[1]), send_sems, recv_sems)
    shape = (3, layers, size_y, summed.shape[3])
    summed = add_ends(
        summed, unpack(x_in[0], shape, lanes), unpack(x_in[1], shape, lanes), 1, width
    )
    y_out[0] = pack(summed[:, :, size_y - layers :, :], lanes)
    y_out[1] = pack(summed[:, :, :layers, :], lanes)
    swap("gy", (y_out.at[0], y_out.at[1]), (y_in.at[0], y_in.at[1]), send_sems, recv_sems)
    shape = (3, summed.shape[1], layers, summed.shape[3])
    out[...] = add_ends(
        summed, unpack(y_in[0], shape, lanes), unpack(y_in[1], shape, lanes), 2, width
    )


def spread_sums(ghosts, width):
    _, size_x, size_y, size_z = ghosts.shape
    more = 2 * (width - 1)
    z_slab = (2, size_x, size_y, 3 * (width + 1))
    x_slab = (2, (3 * (width + 1) + 1) * size_y, size_z - 2)
    y_slab = (2, (3 * (size_x + more) + 1) * (width + 1), size_z - 2)
    return call_kernel(
        functools.partial(spread_kernel, width),
        (ghosts,),
        ((3, size_x + more, size_y + more, size_z + more),),
        [z_slab, z_slab, x_slab, x_slab, y_slab, y_slab],
        width,
    )[0]


def project(vector, direction):
    summed = None
    for d in range(3):
        if direction[d] != 0:
            signed = vector[d] if direction[d] > 0 else -vector[d]
            summed = signed if summed is None else summed + signed
    return summed


def moments(fields):
    density = fields[0]
    for i in range(1, 19):
        density = density + fields[i]
    components = []
    for d in range(3):
        summed = None
        for i in range(1, 19):
            if directions[i][d] != 0:
                signed = fields[i] if directions[i][d] > 0 else -fields[i]
                summed = signed if summed is None else summed + signed
        components.append(summed)
    return (density, jnp.stack(components))


def collide(fields, density, velocity, cell_force, gray_fraction):
    flow_square = velocity[0] * velocity[0] + velocity[1] * velocity[1] + velocity[2] * velocity[2]
    post_list = []
    for i in range(19):
        baseline = density - 1.5 * flow_square
        if i > 0:
            along_flow = project(velocity, directions[i])
            along_force = project(cell_force, directions[i])
            baseline = baseline + 3.0 * along_flow + 4.5 * along_flow * along_flow
        equilibrium = weights[i] * baseline
        relaxed = fields[i] + relax_rate * (equilibrium - fields[i])
        if i > 0:
            relaxed = relaxed + 3.0 * weights[i] * along_force
        post_list.append((1.0 - gray_fraction) * relaxed + gray_fraction * fields[opposite[i]])
    return post_list


def propagate(post_list):
    moved = []
    for i in range(19):
        layer = post_list[i]
        for dim in range(3):
            start = 1 - directions[i][dim]
            layer = lax.slice_in_dim(layer, start, start + layer.shape[dim] - 2, axis=dim)
        moved.append(layer)
    return moved


def per_device(
    populations,
    solid_class,
    part_offset,
    part_velocity,
    part_drag,
    part_cell,
    block_rows,
    block_dest,
):
    size_x, size_y, size_z = (populations.shape[1], populations.shape[2], populations.shape[3])
    rows_block = part_cell.shape[1]
    block_count = block_dest.shape[0]
    peers = lax.axis_size("gx")
    capacity = 2 * block_count // peers
    slot_count = peers * capacity
    destination = block_dest[:, 0]
    onehot = (destination[:, None] == jnp.arange(peers, dtype=jnp.int32)[None, :]).astype(jnp.int32)
    before = jnp.cumsum(onehot, axis=0) - onehot
    block_rank = jnp.sum(before * onehot, axis=1)
    slot_index = destination * capacity + block_rank
    match = slot_index[None, :] == jnp.arange(slot_count, dtype=jnp.int32)[:, None]
    filled = jnp.any(match, axis=1)
    source = jnp.sum(jnp.where(match, jnp.arange(block_count, dtype=jnp.int32)[None, :], 0), axis=1)
    alive = jnp.arange(rows_block, dtype=jnp.int32)[None, :] < block_rows[:, None]
    named = jnp.where(alive, part_cell, -1).astype(jnp.float32)
    floats = jnp.concatenate(
        [part_offset, part_velocity, part_drag[:, None, :], named[:, None, :]], axis=1
    )
    empty = jnp.where(jnp.arange(8) == 7, -1.0, 0.0).astype(jnp.float32)[None, :, None]
    send_floats = jnp.where(filled[:, None, None], jnp.take(floats, source, axis=0), empty)
    wide, got_floats = with_halo(populations, solid_class, send_floats, peers, STEPS)
    offset = got_floats[:, 0:3, :]
    velocity = got_floats[:, 3:6, :]
    drag_rate = got_floats[:, 6, :]
    live_rows = got_floats[:, 7, :] >= 0.0
    got_cells = jnp.maximum(got_floats[:, 7, :], 0.0).astype(jnp.int32)
    p = got_cells // (size_y * size_z) + 1
    q = got_cells // size_z % size_y + 1
    s = got_cells % size_z + 1
    slots = offset.shape[0]
    tables = []
    for d, (place, extent) in enumerate(((p, size_x + 2), (q, size_y + 2), (s, size_z + 2))):
        displace = offset[:, d, :].reshape(-1)
        nearer = place.reshape(-1)
        farther = nearer + jnp.where(displace >= 0.0, 1, -1).astype(jnp.int32)
        grid = jnp.arange(extent, dtype=jnp.int32)[None, :]
        tables.append(
            jnp.where(grid == nearer[:, None], (1.0 - jnp.abs(displace))[:, None], 0.0)
            + jnp.where(grid == farther[:, None], jnp.abs(displace)[:, None], 0.0)
        )
    across = (tables[0][:, :, None] * tables[1][:, None, :]).reshape(slots * rows_block, -1)
    fields = [wide[i] for i in range(19)]
    gray_fraction = wide[19]
    for repeat in range(STEPS):
        reach = STEPS - repeat
        density, flow = moments(fields)
        near = flow
        for d, size in enumerate((size_x, size_y, size_z)):
            near = lax.slice_in_dim(near, reach - 1, reach + 1 + size, axis=d + 1)
        lines = near.reshape(3, -1, size_z + 2)
        along = jnp.einsum("nz,dkz->dnk", tables[2], lines, precision=lax.Precision.HIGH)
        sampled = jnp.sum(along * across[None], axis=2).reshape(3, slots, rows_block)
        sampled = jnp.moveaxis(sampled, 0, 1)
        drag_force = jnp.where(
            live_rows[:, None, :], drag_rate[:, None, :] * (sampled - velocity), 0.0
        )
        velocity = velocity + drag_force
        pushed = -jnp.moveaxis(drag_force, 1, 0).reshape(3, -1)
        ghosts = jnp.einsum(
            "dnk,nz->dkz", pushed[:, :, None] * across[None], tables[2],
            precision=lax.Precision.HIGH,
        )
        ghosts = ghosts.reshape(3, size_x + 2, size_y + 2, size_z + 2)
        cell_force = spread_sums(ghosts, reach)
        post_list = collide(fields, density, flow, cell_force, gray_fraction)
        fields = propagate(post_list)
        gray_fraction = gray_fraction[1:-1, 1:-1, 1:-1]
    density, flow = moments(fields)
    fluid_velocity = flow / speed_unit
    particle_velocity = jnp.where(live_rows[:, None, :], velocity / speed_unit, 0.0)
    return (fluid_velocity, particle_velocity)


def solution(mesh):
    in_specs = (
        P(None, "gx", "gy", "gz"),
        P("gx", "gy", "gz"),
        P(("gx", "gy", "gz"), None, None),
        P(("gx", "gy", "gz"), None, None),
        P(("gx", "gy", "gz"), None),
        P(("gx", "gy", "gz"), None),
        P(("gx", "gy", "gz")),
        P(("gx", "gy", "gz"), None),
    )
    out_specs = (P(None, "gx", "gy", "gz"), P(("gx", "gy", "gz"), None, None))
    return jax.shard_map(
        per_device, mesh=mesh, in_specs=in_specs, out_specs=out_specs, check_vma=False
    )
```
